32 devices in a mesh: groups: 2 (over y), row: 4 (over z), col: 4 (over x, core).
Axes of the slice: x: 2, y: 2, z: 4, core: 2. Of those that a mesh axis runs over, the one named last changes fastest.
Arguments:
- positions: float32 [3, 2048], P(None, ('groups', 'row', 'col')), parts along dimension 1, as said below
- probes: float32 [3, 16, 2048], P(None, None, ('groups', 'row', 'col')), parts along dimension 2, may hold values from -6 to 6
Outputs:
- noise_field: float32 [3, 16, 2048], P(None, None, ('groups', 'row', 'col')), parts along dimension 2
The draws below stay inside these ranges and needn't reach their ends.
There are 2 independent parts, one for each index of `groups`. The reference program is written for one: setup_inputs(seed, part) draws one part's arguments, and reference() takes and returns one part's arrays. A program takes and returns all parts, laid end to end along the dimension named above; each array names one. Nothing has to cross between parts.
Inputs may be any that keep to these rules, and one draw needn't show every extreme that they name: `positions`: beads lie near the points of a lattice of unit spacing, 16 by 16 by 4 layers, bead i near (i % 16, (i // 16) % 16, i // 256), each coordinate within 0.2 of it, so that no two beads are closer than 2 a.
All inputs are finite; a program needn't handle non-finite values.
Results may differ from the reference program's by a relative error of at most 0.0003.
Values sent between devices are 32-bit elements; how exact they have to be, the bound alone decides.
A program may use at most 128 MiB of HBM per device.

```python
import math
import jax
import jax.numpy as jnp
from jax import lax

PROBES = 16
DEG = 4
BEADS = 1024


def draw_positions(key, part):
    bead_ids = jnp.arange(BEADS, dtype=jnp.int32)
    lattice = jnp.stack([bead_ids % 16, bead_ids // 16 % 16, bead_ids // 256]).astype(jnp.float32)
    jitter = jnp.clip(0.08 * jax.random.normal(key, (3, BEADS), jnp.float32), -0.2, 0.2)
    return lattice + jitter


def levels(own_key, shape, cuts, smallest, high):
    factor_of = 1.0
    for axis_at, shards_of in cuts:
        steps = jax.random.uniform(jax.random.fold_in(jax.random.fold_in(own_key, 6), axis_at), (shards_of,), jnp.float32, smallest / len(cuts), high / len(cuts))
        factor_of = factor_of * jnp.repeat(jnp.exp(steps), shape[axis_at] // shards_of).reshape((-1,) + (1,) * (len(shape) - 1 - axis_at))
    return factor_of


def gaussian(rng, dims, scale, limit, cuts=(), kind=jnp.bfloat16):
    values = scale * jax.random.normal(rng, dims, jnp.float32)
    if cuts:
        values = values * levels(rng, dims, cuts, -0.22, 0.18)
    return jnp.clip(values, -limit, limit).astype(kind)


def setup_inputs(seed: int = 0, part: int = 0) -> dict:
    arg_keys = jax.random.split(jax.random.key(seed), 3)
    part_splits = jax.random.split(jax.random.fold_in(arg_keys[2], part), 3)
    positions = draw_positions(jax.random.fold_in(jax.random.fold_in(arg_keys[2], part), 71), part)
    probes = gaussian(part_splits[1], (3, PROBES, BEADS), 1.0, 6.0, ((2, 16),), jnp.float32)
    return dict(positions=positions, probes=probes)


RADIUS = 0.3

def cheb_weight(degree_step):
    if degree_step == 0:
        return 2.0 / math.pi
    return 4.0 * (-1.0) ** (degree_step + 1) / (math.pi * (4.0 * degree_step * degree_step - 1.0))

def mobility_block(rows_pos, rows_ids, cols_pos, cols_ids):
    delta = rows_pos[:, :, None] - cols_pos[:, None, :]
    dist_sq = lax.optimization_barrier(jnp.sum(delta * delta, axis=0))
    same = rows_ids[:, None] == cols_ids[None, :]
    inverse = lax.rsqrt(dist_sq + same.astype(jnp.float32))
    inv_sq = inverse * inverse
    scaled = 0.75 * RADIUS * inverse
    along = jnp.where(same, jnp.float32(1.0), scaled * (1.0 + 2.0 / 3.0 * RADIUS * RADIUS * inv_sq))
    across = jnp.where(same, jnp.float32(0.0), scaled * inv_sq * (1.0 - 2.0 * RADIUS * RADIUS * inv_sq))
    identity = jnp.eye(3, dtype=jnp.float32)
    return identity[:, :, None, None] * along[None, None] + delta[:, None] * (across[None] * delta)[None]

def product(positions, vectors):
    block = math.gcd(BEADS, 256)
    all_ids = jnp.arange(BEADS, dtype=jnp.int32)

    def one_block(index):
        begin_at = (index * block).astype(jnp.int32)
        rows_pos = lax.dynamic_slice_in_dim(positions, begin_at, block, 1)
        rows_ids = lax.dynamic_slice_in_dim(all_ids, begin_at, block, 0)
        mobility = mobility_block(rows_pos, rows_ids, positions, all_ids)
        image = jnp.einsum('abrc,bpc->apr', mobility, vectors, precision=lax.Precision.HIGHEST)
        magnitude = lax.optimization_barrier(jnp.sum(jnp.abs(mobility), axis=(1, 3)))
        return (image, magnitude)
    images, magnitudes = lax.map(one_block, jnp.arange(BEADS // block, dtype=jnp.int32))
    image = jnp.moveaxis(images, 0, 2).reshape(3, PROBES, BEADS)
    row_sums = jnp.moveaxis(magnitudes, 0, 1).reshape(3, BEADS)
    return (image, row_sums)

def reference(positions, probes):
    first_image, row_sums = product(positions, probes)
    ceiling = jnp.max(row_sums)
    factor = 2.0 / ceiling
    previous = probes
    current = factor * first_image - probes
    noise_sum = cheb_weight(0) * previous + cheb_weight(1) * current
    for degree_step in range(2, DEG + 1):
        image, unused = product(positions, current)
        following = 2.0 * (factor * image - current) - previous
        previous, current = (current, following)
        noise_sum = noise_sum + cheb_weight(degree_step) * current
    return jnp.sqrt(ceiling) * noise_sum
```

```python
import functools
import math

import jax
import jax.numpy as jnp
from jax import lax
from jax.experimental import pallas as pl
from jax.experimental.pallas import tpu as pltpu
from jax.sharding import PartitionSpec as P

DEG = 4
RADIUS = 0.3
MESH = pl.DeviceIdType.MESH
F32 = jnp.float32
BF16 = jnp.bfloat16


def cheb_weight(degree_step):
    if degree_step == 0:
        return 2.0 / math.pi
    return 4.0 * (-1.0) ** (degree_step + 1) / (math.pi * (4.0 * degree_step * degree_step - 1.0))


def flip(index, bits):
    for bit in (1, 2, 4, 8):
        if bits & bit:
            index = index + bit - 2 * bit * lax.rem(lax.div(index, bit), 2)
    return index


def split(value):
    high = value.astype(BF16)
    return high, (value - high.astype(F32)).astype(BF16)


def kernel(
    pos_ref, probes_ref, out_ref,
    msg, first, field, posT, w_high, w_low, gather, last_out, last_in,
    first_send, first_recv, gather_send, gather_recv, last_send, last_recv,
):
    row = lax.axis_index("row")
    col = lax.axis_index("col")
    partners = [(dr, dc) for dc in range(4) for dr in (2, 3, 1, 0) if (dr, dc) != (0, 0)]

    barrier = pltpu.get_barrier_semaphore()
    for dr, dc in partners:
        pl.semaphore_signal(
            barrier, inc=1, device_id={"row": flip(row, dr), "col": flip(col, dc)}, device_id_type=MESH
        )

    scaled_pos = pos_ref[...] * (1.0 / (0.75 * RADIUS))
    for r in range(4):
        mine = [probes_ref[t, 4 * r : 4 * r + 4, :] for t in range(3)]
        left = jnp.concatenate([mine[0], mine[1]], axis=0)
        right = jnp.concatenate([mine[2], scaled_pos, jnp.zeros((1, 64), F32)], axis=0)
        msg[r] = jnp.concatenate([left, right], axis=1)
    first[0, 0] = msg[row]

    pl.semaphore_wait(barrier, len(partners))
    first_copies = {}
    for dr, dc in partners:
        to_row = flip(row, dr)
        copy = pltpu.make_async_remote_copy(
            src_ref=msg.at[to_row],
            dst_ref=first.at[dc, dr],
            send_sem=first_send.at[dc, dr],
            recv_sem=first_recv.at[dc, dr],
            device_id={"row": to_row, "col": flip(col, dc)},
            device_id_type=MESH,
        )
        copy.start()
        first_copies[dc, dr] = copy

    low_lanes = lax.broadcasted_iota(jnp.int32, (8, 128), 1) < 64

    for dc in range(4):
        for dr in range(4):
            if (dc, dr) != (0, 0):
                first_copies[dc, dr].wait_recv()
        for h in range(2):
            even, odd = first[dc, 2 * h], first[dc, 2 * h + 1]
            lanes = slice(128 * h, 128 * h + 128)
            field[dc, 0:8, lanes] = jnp.where(low_lanes, even, pltpu.roll(odd, 64, 1))
            field[dc, 8:16, lanes] = jnp.where(low_lanes, pltpu.roll(even, 64, 1), odd)

    stacked = jnp.concatenate(
        [field[dc, 8:16, 128 * h : 128 * h + 128] for dc in range(4) for h in range(2)]
        + [jnp.zeros((64, 128), F32)],
        axis=0,
    )
    posT[...] = stacked.T

    own_pos = [field[0, 12 + t : 13 + t, :] for t in range(3)]
    unit = (0.75 * RADIUS) ** 2
    c_along = 2.0 / 3.0 * RADIUS * RADIUS / unit
    c_across = 2.0 * RADIUS * RADIUS / unit
    STEP = 16
    sums = tuple(jnp.zeros((STEP, 256), F32) for _ in range(3))
    own_bead = lax.broadcasted_iota(jnp.int32, (STEP, 256), 1)
    step_bead = lax.broadcasted_iota(jnp.int32, (STEP, 256), 0)

    for dc in range(4):
        for h in range(2):
            lane = 8 * (2 * dc + h) + 4

            def body(step, sums, dc=dc, h=h, lane=lane):
                at = pl.multiple_of(step * STEP, STEP)
                centres = posT[pl.ds(at, STEP), :]
                d = [own_pos[t] - centres[:, lane + t : lane + t + 1] for t in range(3)]
                dist_sq = d[0] * d[0] + d[1] * d[1] + d[2] * d[2]
                if dc == 0:
                    same = (step_bead + (at + 128 * h)) == own_bead
                    dist_sq = jnp.where(same, 1.0, dist_sq)
                inverse = lax.rsqrt(dist_sq)
                inv_sq = inverse * inverse
                cubed = inverse * inv_sq
                along = inverse + c_along * cubed
                across = cubed - c_across * (cubed * inv_sq)
                if dc == 0:
                    along = jnp.where(same, 1.0, along)
                    across = jnp.where(same, 0.0, across)
                g = [across * d[t] for t in range(3)]
                parts = [
                    along + g[0] * d[0], along + g[1] * d[1], along + g[2] * d[2],
                    g[0] * d[1], g[0] * d[2], g[1] * d[2],
                ]
                mags = [jnp.abs(part) for part in parts]
                rows = pl.ds(pl.multiple_of(128 * h + at, STEP), STEP)
                for k, part in enumerate(parts):
                    high, low = split(part)
                    w_high[dc, rows, 256 * k : 256 * k + 256] = high
                    w_low[dc, rows, 256 * k : 256 * k + 256] = low
                return (
                    sums[0] + (mags[0] + mags[3] + mags[4]),
                    sums[1] + (mags[1] + mags[3] + mags[5]),
                    sums[2] + (mags[2] + mags[4] + mags[5]),
                )

            sums = lax.fori_loop(0, 128 // STEP, body, sums)

    def multiply(block, dc):
        high, low = split(block)
        both = jnp.concatenate([high, low], axis=0)
        image = jnp.dot(both, w_high[dc], preferred_element_type=F32)
        rest = jnp.dot(high, w_low[dc], preferred_element_type=F32)
        return image[0:16] + image[16:32] + rest

    def combine(acc):
        xx, yy, zz, xy, xz, yz = [acc[:, 256 * k : 256 * k + 256] for k in range(6)]
        return jnp.concatenate(
            [
                xx[0:4] + xy[4:8] + xz[8:12],
                xy[0:4] + yy[4:8] + yz[8:12],
                xz[0:4] + yz[4:8] + zz[8:12],
            ],
            axis=0,
        )

    def send(k, value):
        gather[k, 0] = value
        copies = {}
        for dc in (3, 2, 1):
            copy = pltpu.make_async_remote_copy(
                src_ref=gather.at[k, 0],
                dst_ref=gather.at[k, dc],
                send_sem=gather_send.at[k, dc],
                recv_sem=gather_recv.at[k, dc],
                device_id={"row": row, "col": flip(col, dc)},
                device_id_type=MESH,
            )
            copy.start()
            copies[dc] = copy
        return copies

    def apply(k, copies):
        acc = multiply(gather[k, 0], 0)
        for dc in range(1, 4):
            copies[dc].wait_recv()
            acc = acc + multiply(gather[k, dc], dc)
        return combine(acc)

    acc = multiply(field[0], 0)
    for dc in range(1, 4):
        acc = acc + multiply(field[dc], dc)
    image1 = combine(acc)
    row_max = functools.reduce(
        jnp.maximum, [jnp.max(jnp.sum(s, axis=0, keepdims=True), axis=1, keepdims=True) for s in sums]
    )
    copies1 = send(0, jnp.concatenate([image1, jnp.broadcast_to(row_max, (4, 256))], axis=0))
    image2 = apply(0, copies1)
    top = functools.reduce(jnp.maximum, [gather[0, dc, 12:13, :] for dc in range(4)])
    factor = 2.0 / top
    start = field[0, 0:12, :]
    basis1 = factor * image1 - start
    basis2 = 2.0 * (factor * (factor * image2 - image1) - basis1) - start
    pad = jnp.zeros((4, 256), F32)
    copies2 = send(1, jnp.concatenate([basis2, pad], axis=0))
    basis3 = 2.0 * (factor * apply(1, copies2) - basis2) - basis1
    copies3 = send(2, jnp.concatenate([basis3, pad], axis=0))
    noise = cheb_weight(0) * start + cheb_weight(1) * basis1
    noise = noise + cheb_weight(2) * basis2 + cheb_weight(3) * basis3
    basis4 = 2.0 * (factor * apply(2, copies3) - basis3) - basis2
    noise = jnp.sqrt(top) * (noise + cheb_weight(4) * basis4)

    noise = jnp.concatenate([noise, pad], axis=0)
    last_copies = []
    for dr in (2, 3, 1, 0):
        h = dr // 2
        upper = noise[0:8, 128 * h : 128 * h + 128]
        lower = noise[8:16, 128 * h : 128 * h + 128]
        if dr % 2 == 0:
            tile = jnp.where(low_lanes, upper, pltpu.roll(lower, 64, 1))
        else:
            tile = jnp.where(low_lanes, pltpu.roll(upper, 64, 1), lower)
        if dr == 0:
            last_in[row] = tile
        else:
            last_out[dr] = tile
            copy = pltpu.make_async_remote_copy(
                src_ref=last_out.at[dr],
                dst_ref=last_in.at[row],
                send_sem=last_send.at[dr],
                recv_sem=last_recv.at[dr],
                device_id={"row": flip(row, dr), "col": col},
                device_id_type=MESH,
            )
            copy.start()
            last_copies.append(copy)
    for copy in list(first_copies.values()):
        copy.wait_send()
    for copies in (copies1, copies2, copies3):
        for copy in copies.values():
            copy.wait_send()
    for copy in last_copies:
        copy.wait()
    for q in range(4):
        tile = last_in[q]
        out_ref[0, 4 * q : 4 * q + 4, :] = tile[0:4, 0:64]
        out_ref[1, 4 * q : 4 * q + 4, :] = tile[4:8, 0:64]
        out_ref[2, 4 * q : 4 * q + 4, :] = tile[0:4, 64:128]


def fused(positions, probes):
    DMA = pltpu.SemaphoreType.DMA
    return pl.pallas_call(
        kernel,
        out_shape=jax.ShapeDtypeStruct(probes.shape, F32),
        in_specs=[pl.BlockSpec(memory_space=pltpu.VMEM)] * 2,
        out_specs=pl.BlockSpec(memory_space=pltpu.VMEM),
        scratch_shapes=[
            pltpu.VMEM((4, 8, 128), F32),
            pltpu.VMEM((4, 4, 8, 128), F32),
            pltpu.VMEM((4, 16, 256), F32),
            pltpu.VMEM((128, 128), F32),
            pltpu.VMEM((4, 256, 1536), BF16),
            pltpu.VMEM((4, 256, 1536), BF16),
            pltpu.VMEM((DEG - 1, 4, 16, 256), F32),
            pltpu.VMEM((4, 8, 128), F32),
            pltpu.VMEM((4, 8, 128), F32),
            DMA((4, 4)),
            DMA((4, 4)),
            DMA((DEG - 1, 4)),
            DMA((DEG - 1, 4)),
            DMA((4,)),
            DMA((4,)),
        ],
        compiler_params=pltpu.CompilerParams(
            collective_id=0, has_side_effects=True, vmem_limit_bytes=32 * 1024 * 1024
        ),
        name="fused",
    )(positions, probes)


def block_width(length):
    width = min(length, 512)
    while length % width != 0:
        width = width - 1
    return width


def mobility_block(rows_pos, rows_ids, cols_pos, cols_ids):
    delta = rows_pos[:, :, None] - cols_pos[:, None, :]
    dist_sq = jnp.sum(delta * delta, axis=0)
    same = rows_ids[:, None] == cols_ids[None, :]
    inverse = lax.rsqrt(dist_sq + same.astype(jnp.float32))
    inv_sq = inverse * inverse
    scaled = 0.75 * RADIUS * inverse
    along = jnp.where(same, jnp.float32(1.0), scaled * (1.0 + 2.0 / 3.0 * RADIUS * RADIUS * inv_sq))
    across = jnp.where(
        same, jnp.float32(0.0), scaled * inv_sq * (1.0 - 2.0 * RADIUS * RADIUS * inv_sq)
    )
    identity = jnp.eye(3, dtype=jnp.float32)
    return (
        identity[:, :, None, None] * along[None, None]
        + delta[:, None] * (across[None] * delta)[None]
    )


def gathered(positions, probes):
    seg_len = positions.shape[1]
    probe_count = probes.shape[1]
    n_row = lax.axis_size("row")
    n_col = lax.axis_size("col")
    beads_all = seg_len * n_row * n_col
    places = lax.all_gather(positions, ("row", "col"), axis=1, tiled=True)
    all_ids = jnp.arange(beads_all, dtype=jnp.int32)
    own_at = (lax.axis_index("row") * n_col + lax.axis_index("col")) * seg_len
    own_ids = own_at + jnp.arange(seg_len, dtype=jnp.int32)
    width = block_width(beads_all)

    def apply_mobility(vectors):
        whole = lax.all_gather(vectors, ("row", "col"), axis=2, tiled=True)

        def add_block(block_step, carried):
            offset = block_step * width
            cols_pos = lax.dynamic_slice_in_dim(places, offset, width, 1)
            cols_ids = lax.dynamic_slice_in_dim(all_ids, offset, width, 0)
            mobility = mobility_block(positions, own_ids, cols_pos, cols_ids)
            columns = lax.dynamic_slice_in_dim(whole, offset, width, 2)
            image = carried[0] + jnp.einsum(
                "abrc,bpc->apr", mobility, columns, precision=lax.Precision.HIGHEST
            )
            return image, carried[1] + jnp.sum(jnp.abs(mobility), axis=(1, 3))

        zeros = (jnp.zeros((3, probe_count, seg_len), F32), jnp.zeros((3, seg_len), F32))
        return lax.fori_loop(0, beads_all // width, add_block, zeros)

    image, row_sums = apply_mobility(probes)
    ceiling = lax.pmax(jnp.max(row_sums), ("row", "col"))
    factor = 2.0 / ceiling
    previous = probes
    current = factor * image - probes
    noise_sum = cheb_weight(0) * previous + cheb_weight(1) * current
    for degree_step in range(2, DEG + 1):
        following = 2.0 * (factor * apply_mobility(current)[0] - current) - previous
        previous, current = (current, following)
        noise_sum = noise_sum + cheb_weight(degree_step) * current
    return jnp.sqrt(ceiling) * noise_sum


def solution(mesh):
    split_by = ("groups", "row", "col")
    square = mesh.shape["row"] == 4 and mesh.shape["col"] == 4

    def per_device(positions, probes):
        if square and probes.shape == (3, 16, 64):
            return fused(positions, probes)
        return gathered(positions, probes)

    return jax.shard_map(
        per_device,
        mesh=mesh,
        in_specs=(P(None, split_by), P(None, None, split_by)),
        out_specs=P(None, None, split_by),
        check_vma=False,
    )
```

```python
import functools
import math

import jax
import jax.numpy as jnp
from jax import lax
from jax.experimental import pallas as pl
from jax.experimental.pallas import tpu as pltpu
from jax.sharding import PartitionSpec as P

DEG = 4
RADIUS = 0.3
MESH = pl.DeviceIdType.MESH
F32 = jnp.float32
BF16 = jnp.bfloat16


def cheb_weight(degree_step):
    if degree_step == 0:
        return 2.0 / math.pi
    return 4.0 * (-1.0) ** (degree_step + 1) / (math.pi * (4.0 * degree_step * degree_step - 1.0))


def flip(index, bits):
    for bit in (1, 2, 4, 8):
        if bits & bit:
            index = index + bit - 2 * bit * lax.rem(lax.div(index, bit), 2)
    return index


def split(value):
    high = value.astype(BF16)
    return high, (value - high.astype(F32)).astype(BF16)


def kernel(
    pos_hbm, probes_hbm, out_ref,
    pos_ref, probes_ref, msg, first, field, posT, w_high, w_low, gather, last_out, last_in,
    load, first_send, first_recv, gather_send, gather_recv, last_send, last_recv,
):
    row = lax.axis_index("row")
    col = lax.axis_index("col")
    partners = [(dr, dc) for dc in range(4) for dr in (2, 3, 1, 0) if (dr, dc) != (0, 0)]

    loads = [
        pltpu.make_async_copy(pos_hbm, pos_ref, load.at[0]),
        pltpu.make_async_copy(probes_hbm, probes_ref, load.at[1]),
    ]
    for copy in loads:
        copy.start()
    barrier = pltpu.get_barrier_semaphore()
    for dr, dc in partners:
        pl.semaphore_signal(
            barrier, inc=1, device_id={"row": flip(row, dr), "col": flip(col, dc)}, device_id_type=MESH
        )
    for copy in loads:
        copy.wait()

    scaled_pos = pos_ref[...] * (1.0 / (0.75 * RADIUS))
    for r in range(4):
        mine = [probes_ref[t, 4 * r : 4 * r + 4, :] for t in range(3)]
        left = jnp.concatenate([mine[0], mine[1]], axis=0)
        right = jnp.concatenate([mine[2], scaled_pos, jnp.zeros((1, 64), F32)], axis=0)
        msg[r] = jnp.concatenate([left, right], axis=1)
    first[0, 0] = msg[row]

    pl.semaphore_wait(barrier, len(partners))
    first_copies = {}
    for dr, dc in partners:
        to_row = flip(row, dr)
        copy = pltpu.make_async_remote_copy(
            src_ref=msg.at[to_row],
            dst_ref=first.at[dc, dr],
            send_sem=first_send.at[dc, dr],
            recv_sem=first_recv.at[dc, dr],
            device_id={"row": to_row, "col": flip(col, dc)},
            device_id_type=MESH,
        )
        copy.start()
        first_copies[dc, dr] = copy

    low_lanes = lax.broadcasted_iota(jnp.int32, (8, 128), 1) < 64

    def unpack(dc):
        for h in range(2):
            even, odd = first[dc, 2 * h], first[dc, 2 * h + 1]
            lanes = slice(128 * h, 128 * h + 128)
            field[dc, 0:8, lanes] = jnp.where(low_lanes, even, pltpu.roll(odd, 64, 1))
            field[dc, 8:16, lanes] = jnp.where(low_lanes, pltpu.roll(even, 64, 1), odd)
        pair = jnp.concatenate([field[dc, 8:16, 0:128], field[dc, 8:16, 128:256]], axis=0)
        posT[dc] = pair.T

    unit = (0.75 * RADIUS) ** 2
    c_along = 2.0 / 3.0 * RADIUS * RADIUS / unit
    c_across = 2.0 * RADIUS * RADIUS / unit
    STEP = 16
    own_bead = lax.broadcasted_iota(jnp.int32, (STEP, 128), 1)
    step_bead = lax.broadcasted_iota(jnp.int32, (STEP, 128), 0)
    sums = [[jnp.zeros((8, 128), F32) for _ in range(3)] for _ in range(2)]

    def generate(dc, h):
        for at in range(0, 128, STEP):
            rows = slice(128 * h + at, 128 * h + at + STEP)
            centres = [posT[dc, at : at + STEP, 8 * h + 4 + t : 8 * h + 5 + t] for t in range(3)]
            centres = [jnp.broadcast_to(c, (STEP, 128)) for c in centres]
            for own in range(2):
                d = [field[0, 12 + t : 13 + t, 128 * own : 128 * own + 128] - centres[t] for t in range(3)]
                dist_sq = d[0] * d[0] + d[1] * d[1] + d[2] * d[2]
                diagonal = dc == 0 and own == h
                if diagonal:
                    same = (step_bead + at) == own_bead
                    dist_sq = jnp.where(same, 1.0, dist_sq)
                inverse = lax.rsqrt(dist_sq)
                inv_sq = inverse * inverse
                cubed = inverse * inv_sq
                along = inverse + c_along * cubed
                across = cubed - c_across * (cubed * inv_sq)
                if diagonal:
                    along = jnp.where(same, 1.0, along)
                    across = jnp.where(same, 0.0, across)
                g = [across * d[t] for t in range(3)]
                parts = [
                    along + g[0] * d[0], along + g[1] * d[1], along + g[2] * d[2],
                    g[0] * d[1], g[0] * d[2], g[1] * d[2],
                ]
                for k, part in enumerate(parts):
                    high, low = split(part)
                    lanes = slice(768 * own + 128 * k, 768 * own + 128 * k + 128)
                    w_high[dc, rows, lanes] = high
                    w_low[dc, rows, lanes] = low
                mags = [jnp.abs(part) for part in parts]
                mags = [mag[0:8] + mag[8:16] for mag in mags]
                for t, (p, q, r) in enumerate(((0, 3, 4), (1, 3, 5), (2, 4, 5))):
                    sums[own][t] = sums[own][t] + (mags[p] + mags[q] + mags[r])

    def multiply(block, dc):
        high, low = split(block)
        both = jnp.concatenate([high, low], axis=0)
        image = jnp.dot(both, w_high[dc], preferred_element_type=F32)
        rest = jnp.dot(high, w_low[dc], preferred_element_type=F32)
        return image[0:16] + image[16:32] + rest

    def combine(acc):
        halves = []
        for own in range(2):
            xx, yy, zz, xy, xz, yz = [
                acc[:, 768 * own + 128 * k : 768 * own + 128 * k + 128] for k in range(6)
            ]
            halves.append(
                jnp.concatenate(
                    [
                        xx[0:4] + xy[4:8] + xz[8:12],
                        xy[0:4] + yy[4:8] + yz[8:12],
                        xz[0:4] + yz[4:8] + zz[8:12],
                    ],
                    axis=0,
                )
            )
        return jnp.concatenate(halves, axis=1)

    def send(k, value):
        gather[k, 0] = value
        copies = {}
        for dc in (3, 2, 1):
            copy = pltpu.make_async_remote_copy(
                src_ref=gather.at[k, 0],
                dst_ref=gather.at[k, dc],
                send_sem=gather_send.at[k, dc],
                recv_sem=gather_recv.at[k, dc],
                device_id={"row": row, "col": flip(col, dc)},
                device_id_type=MESH,
            )
            copy.start()
            copies[dc] = copy
        return copies

    def apply(k, copies):
        acc = multiply(gather[k, 0], 0)
        for dc in range(1, 4):
            copies[dc].wait_recv()
            acc = acc + multiply(gather[k, dc], dc)
        return combine(acc)

    for dr in (2, 3, 1):
        first_copies[0, dr].wait_recv()
    unpack(0)
    generate(0, 0)
    generate(0, 1)
    for dc in range(1, 4):
        for dr in range(4):
            first_copies[dc, dr].wait_recv()
    for dc in range(1, 4):
        unpack(dc)
    acc = None
    for dc in range(1, 4):
        generate(dc, 0)
        term = multiply(field[dc - 1], dc - 1)
        acc = term if acc is None else acc + term
        generate(dc, 1)
    acc = acc + multiply(field[3], 3)
    image1 = combine(acc)
    row_max = functools.reduce(jnp.maximum, [jnp.sum(s, axis=0, keepdims=True) for half in sums for s in half])
    row_max = jnp.max(row_max, axis=1, keepdims=True)
    copies1 = send(0, jnp.concatenate([image1, jnp.broadcast_to(row_max, (4, 256))], axis=0))
    image2 = apply(0, copies1)
    top = functools.reduce(jnp.maximum, [gather[0, dc, 12:13, :] for dc in range(4)])
    factor = 2.0 / top
    start = field[0, 0:12, :]
    basis1 = factor * image1 - start
    basis2 = 2.0 * (factor * (factor * image2 - image1) - basis1) - start
    pad = jnp.zeros((4, 256), F32)
    copies2 = send(1, jnp.concatenate([basis2, pad], axis=0))
    basis3 = 2.0 * (factor * apply(1, copies2) - basis2) - basis1
    copies3 = send(2, jnp.concatenate([basis3, pad], axis=0))
    noise = cheb_weight(0) * start + cheb_weight(1) * basis1
    noise = noise + cheb_weight(2) * basis2 + cheb_weight(3) * basis3
    basis4 = 2.0 * (factor * apply(2, copies3) - basis3) - basis2
    noise = jnp.sqrt(top) * (noise + cheb_weight(4) * basis4)

    noise = jnp.concatenate([noise, pad], axis=0)
    last_copies = []
    for dr in (2, 3, 1, 0):
        h = dr // 2
        upper = noise[0:8, 128 * h : 128 * h + 128]
        lower = noise[8:16, 128 * h : 128 * h + 128]
        if dr % 2 == 0:
            tile = jnp.where(low_lanes, upper, pltpu.roll(lower, 64, 1))
        else:
            tile = jnp.where(low_lanes, pltpu.roll(upper, 64, 1), lower)
        if dr == 0:
            last_in[row] = tile
        else:
            last_out[dr] = tile
            copy = pltpu.make_async_remote_copy(
                src_ref=last_out.at[dr],
                dst_ref=last_in.at[row],
                send_sem=last_send.at[dr],
                recv_sem=last_recv.at[dr],
                device_id={"row": flip(row, dr), "col": col},
                device_id_type=MESH,
            )
            copy.start()
            last_copies.append(copy)
    for copy in list(first_copies.values()):
        copy.wait_send()
    for copies in (copies1, copies2, copies3):
        for copy in copies.values():
            copy.wait_send()
    for copy in last_copies:
        copy.wait()
    for q in range(4):
        tile = last_in[q]
        out_ref[0, 4 * q : 4 * q + 4, :] = tile[0:4, 0:64]
        out_ref[1, 4 * q : 4 * q + 4, :] = tile[4:8, 0:64]
        out_ref[2, 4 * q : 4 * q + 4, :] = tile[0:4, 64:128]


def fused(positions, probes):
    DMA = pltpu.SemaphoreType.DMA
    return pl.pallas_call(
        kernel,
        out_shape=jax.ShapeDtypeStruct(probes.shape, F32),
        in_specs=[pl.BlockSpec(memory_space=pltpu.HBM)] * 2,
        out_specs=pl.BlockSpec(memory_space=pltpu.VMEM),
        scratch_shapes=[
            pltpu.VMEM(positions.shape, F32),
            pltpu.VMEM(probes.shape, F32),
            pltpu.VMEM((4, 8, 128), F32),
            pltpu.VMEM((4, 4, 8, 128), F32),
            pltpu.VMEM((4, 16, 256), F32),
            pltpu.VMEM((4, 128, 16), F32),
            pltpu.VMEM((4, 256, 1536), BF16),
            pltpu.VMEM((4, 256, 1536), BF16),
            pltpu.VMEM((DEG - 1, 4, 16, 256), F32),
            pltpu.VMEM((4, 8, 128), F32),
            pltpu.VMEM((4, 8, 128), F32),
            DMA((2,)),
            DMA((4, 4)),
            DMA((4, 4)),
            DMA((DEG - 1, 4)),
            DMA((DEG - 1, 4)),
            DMA((4,)),
            DMA((4,)),
        ],
        compiler_params=pltpu.CompilerParams(
            collective_id=0, has_side_effects=True, vmem_limit_bytes=62 * 1024 * 1024
        ),
        name="fused",
    )(positions, probes)


def block_width(length):
    width = min(length, 512)
    while length % width != 0:
        width = width - 1
    return width


def mobility_block(rows_pos, rows_ids, cols_pos, cols_ids):
    delta = rows_pos[:, :, None] - cols_pos[:, None, :]
    dist_sq = jnp.sum(delta * delta, axis=0)
    same = rows_ids[:, None] == cols_ids[None, :]
    inverse = lax.rsqrt(dist_sq + same.astype(jnp.float32))
    inv_sq = inverse * inverse
    scaled = 0.75 * RADIUS * inverse
    along = jnp.where(same, jnp.float32(1.0), scaled * (1.0 + 2.0 / 3.0 * RADIUS * RADIUS * inv_sq))
    across = jnp.where(
        same, jnp.float32(0.0), scaled * inv_sq * (1.0 - 2.0 * RADIUS * RADIUS * inv_sq)
    )
    identity = jnp.eye(3, dtype=jnp.float32)
    return (
        identity[:, :, None, None] * along[None, None]
        + delta[:, None] * (across[None] * delta)[None]
    )


def gathered(positions, probes):
    seg_len = positions.shape[1]
    probe_count = probes.shape[1]
    n_row = lax.axis_size("row")
    n_col = lax.axis_size("col")
    beads_all = seg_len * n_row * n_col
    places = lax.all_gather(positions, ("row", "col"), axis=1, tiled=True)
    all_ids = jnp.arange(beads_all, dtype=jnp.int32)
    own_at = (lax.axis_index("row") * n_col + lax.axis_index("col")) * seg_len
    own_ids = own_at + jnp.arange(seg_len, dtype=jnp.int32)
    width = block_width(beads_all)

    def apply_mobility(vectors):
        whole = lax.all_gather(vectors, ("row", "col"), axis=2, tiled=True)

        def add_block(block_step, carried):
            offset = block_step * width
            cols_pos = lax.dynamic_slice_in_dim(places, offset, width, 1)
            cols_ids = lax.dynamic_slice_in_dim(all_ids, offset, width, 0)
            mobility = mobility_block(positions, own_ids, cols_pos, cols_ids)
            columns = lax.dynamic_slice_in_dim(whole, offset, width, 2)
            image = carried[0] + jnp.einsum(
                "abrc,bpc->apr", mobility, columns, precision=lax.Precision.HIGHEST
            )
            return image, carried[1] + jnp.sum(jnp.abs(mobility), axis=(1, 3))

        zeros = (jnp.zeros((3, probe_count, seg_len), F32), jnp.zeros((3, seg_len), F32))
        return lax.fori_loop(0, beads_all // width, add_block, zeros)

    image, row_sums = apply_mobility(probes)
    ceiling = lax.pmax(jnp.max(row_sums), ("row", "col"))
    factor = 2.0 / ceiling
    previous = probes
    current = factor * image - probes
    noise_sum = cheb_weight(0) * previous + cheb_weight(1) * current
    for degree_step in range(2, DEG + 1):
        following = 2.0 * (factor * apply_mobility(current)[0] - current) - previous
        previous, current = (current, following)
        noise_sum = noise_sum + cheb_weight(degree_step) * current
    return jnp.sqrt(ceiling) * noise_sum


def solution(mesh):
    split_by = ("groups", "row", "col")
    square = mesh.shape["row"] == 4 and mesh.shape["col"] == 4

    def per_device(positions, probes):
        if square and probes.shape == (3, 16, 64):
            return fused(positions, probes)
        return gathered(positions, probes)

    return jax.shard_map(
        per_device,
        mesh=mesh,
        in_specs=(P(None, split_by), P(None, None, split_by)),
        out_specs=P(None, None, split_by),
        check_vma=False,
    )
```

```python
import functools
import math

import jax
import jax.numpy as jnp
from jax import lax
from jax.experimental import pallas as pl
from jax.experimental.pallas import tpu as pltpu
from jax.sharding import PartitionSpec as P

DEG = 4
RADIUS = 0.3
MESH = pl.DeviceIdType.MESH
F32 = jnp.float32
BF16 = jnp.bfloat16


def cheb_weight(degree_step):
    if degree_step == 0:
        return 2.0 / math.pi
    return 4.0 * (-1.0) ** (degree_step + 1) / (math.pi * (4.0 * degree_step * degree_step - 1.0))


def flip(index, bits):
    for bit in (1, 2, 4, 8):
        if bits & bit:
            index = index + bit - 2 * bit * lax.rem(lax.div(index, bit), 2)
    return index


def split(value):
    high = value.astype(BF16)
    return high, (value - high.astype(F32)).astype(BF16)


def kernel(
    pos_hbm, probes_hbm, out_ref,
    pos_ref, probes_ref, msg, first, field, posT, w_high, w_low, gather, last_out, last_in,
    load, row_send, row_recv, first_send, first_recv, gather_send, gather_recv, last_send, last_recv,
):
    row = lax.axis_index("row")
    col = lax.axis_index("col")
    partners = [(2, 0), (3, 0), (1, 0), (0, 2), (0, 3), (0, 1)]

    loads = [
        pltpu.make_async_copy(pos_hbm, pos_ref, load.at[0]),
        pltpu.make_async_copy(probes_hbm, probes_ref, load.at[1]),
    ]
    for copy in loads:
        copy.start()
    barrier = pltpu.get_barrier_semaphore()
    for dr, dc in partners:
        pl.semaphore_signal(
            barrier, inc=1, device_id={"row": flip(row, dr), "col": flip(col, dc)}, device_id_type=MESH
        )
    for copy in loads:
        copy.wait()

    scaled_pos = pos_ref[...] * (1.0 / (0.75 * RADIUS))
    for r in range(4):
        mine = [probes_ref[t, 4 * r : 4 * r + 4, :] for t in range(3)]
        left = jnp.concatenate([mine[0], mine[1]], axis=0)
        right = jnp.concatenate([mine[2], scaled_pos, jnp.zeros((1, 64), F32)], axis=0)
        msg[r] = jnp.concatenate([left, right], axis=1)
    first[0, 0] = msg[row]

    pl.semaphore_wait(barrier, len(partners))
    row_copies = {}
    for dr in (2, 3, 1):
        to_row = flip(row, dr)
        row_copies[dr] = pltpu.make_async_remote_copy(
            src_ref=msg.at[to_row],
            dst_ref=first.at[0, dr],
            send_sem=row_send.at[dr],
            recv_sem=row_recv.at[dr],
            device_id={"row": to_row, "col": col},
            device_id_type=MESH,
        )
        row_copies[dr].start()

    def to_col(source, target, dc, send_sem, recv_sem):
        copy = pltpu.make_async_remote_copy(
            src_ref=source,
            dst_ref=target,
            send_sem=send_sem,
            recv_sem=recv_sem,
            device_id={"row": row, "col": flip(col, dc)},
            device_id_type=MESH,
        )
        copy.start()
        return copy

    low_lanes = lax.broadcasted_iota(jnp.int32, (8, 128), 1) < 64

    def unpack(dc):
        for h in range(2):
            even, odd = first[dc, 2 * h], first[dc, 2 * h + 1]
            field[dc, h, 0:8] = jnp.where(low_lanes, even, pltpu.roll(odd, 64, 1))
            field[dc, h, 8:16] = jnp.where(low_lanes, pltpu.roll(even, 64, 1), odd)
        pair = jnp.concatenate([field[dc, 0, 8:16], field[dc, 1, 8:16]], axis=0)
        posT[dc] = pair.T

    pairs = [((0, 0), (0, 1)), ((1, 1), (2, 1)), ((3, 1), (1, 0)), ((2, 0), (3, 0))]
    place = {half: (block, at) for block, pair in enumerate(pairs) for at, half in enumerate(pair)}

    unit = (0.75 * RADIUS) ** 2
    c_along = 2.0 / 3.0 * RADIUS * RADIUS / unit
    c_across = 2.0 * RADIUS * RADIUS / unit
    STEP = 16
    own_bead = lax.broadcasted_iota(jnp.int32, (STEP, 128), 1)
    step_bead = lax.broadcasted_iota(jnp.int32, (STEP, 128), 0)
    sums = [[jnp.zeros((8, 128), F32) for _ in range(3)] for _ in range(2)]

    def generate(dc, h):
        block, part_at = place[dc, h]
        for at in range(0, 128, STEP):
            rows = slice(128 * part_at + at, 128 * part_at + at + STEP)
            centres = [posT[dc, at : at + STEP, 8 * h + 4 + t : 8 * h + 5 + t] for t in range(3)]
            centres = [jnp.broadcast_to(c, (STEP, 128)) for c in centres]
            for own in range(2):
                d = [field[0, own, 12 + t : 13 + t, :] - centres[t] for t in range(3)]
                dist_sq = d[0] * d[0] + d[1] * d[1] + d[2] * d[2]
                diagonal = dc == 0 and own == h
                if diagonal:
                    same = (step_bead + at) == own_bead
                    dist_sq = jnp.where(same, 1.0, dist_sq)
                inverse = lax.rsqrt(dist_sq)
                inv_sq = inverse * inverse
                cubed = inverse * inv_sq
                along = inverse + c_along * cubed
                across = cubed - c_across * (cubed * inv_sq)
                if diagonal:
                    along = jnp.where(same, 1.0, along)
                    across = jnp.where(same, 0.0, across)
                g = [across * d[t] for t in range(3)]
                parts = [
                    along + g[0] * d[0], along + g[1] * d[1], along + g[2] * d[2],
                    g[0] * d[1], g[0] * d[2], g[1] * d[2],
                ]
                for k, part in enumerate(parts):
                    high, low = split(part)
                    lanes = slice(768 * own + 128 * k, 768 * own + 128 * k + 128)
                    w_high[block, rows, lanes] = high
                    w_low[block, rows, lanes] = low
                mags = [jnp.abs(part) for part in parts]
                mags = [mag[0:8] + mag[8:16] for mag in mags]
                for t, (p, q, r) in enumerate(((0, 3, 4), (1, 3, 5), (2, 4, 5))):
                    sums[own][t] = sums[own][t] + (mags[p] + mags[q] + mags[r])

    def multiply(parts, block, own):
        high, low = parts
        lanes = slice(768 * own, 768 * own + 768)
        both = jnp.concatenate([high, low], axis=0)
        image = jnp.dot(both, w_high[block, :, lanes], preferred_element_type=F32)
        rest = jnp.dot(high, w_low[block, :, lanes], preferred_element_type=F32)
        return image[0:16] + image[16:32] + rest

    def combine(acc):
        xx, yy, zz, xy, xz, yz = [acc[:, 128 * k : 128 * k + 128] for k in range(6)]
        return jnp.concatenate(
            [
                xx[0:4] + xy[4:8] + xz[8:12],
                xy[0:4] + yy[4:8] + yz[8:12],
                xz[0:4] + yz[4:8] + zz[8:12],
            ],
            axis=0,
        )

    def operand(halves, block):
        return split(jnp.concatenate([halves(*half) for half in pairs[block]], axis=1))

    gather_copies = {}

    def send(k, own, value, rest):
        gather[k, 0, own] = jnp.concatenate([value, rest], axis=0)
        for dc in (2, 3, 1):
            gather_copies[k, dc, own] = to_col(
                gather.at[k, 0, own], gather.at[k, dc, own], dc,
                gather_send.at[k, dc, own], gather_recv.at[k, dc, own],
            )

    def images(k):
        acc = [None, None]
        for block in range(4):
            for dc, h in pairs[block]:
                if dc:
                    gather_copies[k, dc, h].wait_recv()
            parts = operand(lambda dc, h: gather[k, dc, h], block)
            for own in (1, 0):
                term = multiply(parts, block, own)
                acc[own] = term if block == 0 else acc[own] + term
                if block == 3:
                    yield own, combine(acc[own])

    for dr in (1, 2, 3):
        row_copies[dr].wait_recv()
    first_copies = [
        to_col(first.at[0], first.at[dc], dc, first_send.at[dc], first_recv.at[dc]) for dc in (2, 3, 1)
    ]
    unpack(0)
    generate(0, 0)
    generate(0, 1)
    for copy in first_copies:
        copy.wait_recv()
    for dc in range(1, 4):
        unpack(dc)

    def field_half(dc, h):
        return field[dc, h]

    acc = [None, None]
    for block in range(4):
        if block < 3:
            generate(*pairs[block + 1][0])
        else:
            row_max = functools.reduce(
                jnp.maximum, [jnp.sum(s, axis=0, keepdims=True) for half in sums for s in half]
            )
            row_max = jnp.broadcast_to(jnp.max(row_max, axis=1, keepdims=True), (4, 128))
        parts = operand(field_half, block)
        for own in (1, 0):
            term = multiply(parts, block, own)
            acc[own] = term if block == 0 else acc[own] + term
            if block == 3:
                acc[own] = combine(acc[own])
                send(0, own, acc[own], row_max)
        if block < 3:
            generate(*pairs[block + 1][1])
    image1 = acc

    pad = jnp.zeros((4, 128), F32)
    start = [field[0, own, 0:12, :] for own in range(2)]
    basis1, basis2, basis3, noise = [None, None], [None, None], [None, None], [None, None]
    factor = top = None
    for own, image2 in images(0):
        if factor is None:
            top = functools.reduce(jnp.maximum, [gather[0, dc, 1, 12:13, :] for dc in range(4)])
            factor = 2.0 / top
        basis1[own] = factor * image1[own] - start[own]
        basis2[own] = 2.0 * (factor * (factor * image2 - image1[own]) - basis1[own]) - start[own]
        send(1, own, basis2[own], pad)
    for own, image3 in images(1):
        basis3[own] = 2.0 * (factor * image3 - basis2[own]) - basis1[own]
        send(2, own, basis3[own], pad)
    for own in range(2):
        noise[own] = cheb_weight(0) * start[own] + cheb_weight(1) * basis1[own]
        noise[own] = noise[own] + cheb_weight(2) * basis2[own] + cheb_weight(3) * basis3[own]

    last_copies = []
    root = jnp.sqrt(top)
    for own, image4 in images(2):
        basis4 = 2.0 * (factor * image4 - basis3[own]) - basis2[own]
        result = root * (noise[own] + cheb_weight(4) * basis4)
        upper, lower = result[0:8], jnp.concatenate([result[8:12], pad], axis=0)
        for dr in (2 * own, 2 * own + 1):
            if dr % 2 == 0:
                tile = jnp.where(low_lanes, upper, pltpu.roll(lower, 64, 1))
            else:
                tile = jnp.where(low_lanes, pltpu.roll(upper, 64, 1), lower)
            if dr == 0:
                last_in[row] = tile
                continue
            last_out[dr] = tile
            copy = pltpu.make_async_remote_copy(
                src_ref=last_out.at[dr],
                dst_ref=last_in.at[row],
                send_sem=last_send.at[dr],
                recv_sem=last_recv.at[dr],
                device_id={"row": flip(row, dr), "col": col},
                device_id_type=MESH,
            )
            copy.start()
            last_copies.append(copy)
    for copy in [*row_copies.values(), *first_copies, *gather_copies.values()]:
        copy.wait_send()
    for copy in last_copies:
        copy.wait()
    for q in range(4):
        tile = last_in[q]
        out_ref[0, 4 * q : 4 * q + 4, :] = tile[0:4, 0:64]
        out_ref[1, 4 * q : 4 * q + 4, :] = tile[4:8, 0:64]
        out_ref[2, 4 * q : 4 * q + 4, :] = tile[0:4, 64:128]


def fused(positions, probes):
    DMA = pltpu.SemaphoreType.DMA
    return pl.pallas_call(
        kernel,
        out_shape=jax.ShapeDtypeStruct(probes.shape, F32),
        in_specs=[pl.BlockSpec(memory_space=pltpu.HBM)] * 2,
        out_specs=pl.BlockSpec(memory_space=pltpu.VMEM),
        scratch_shapes=[
            pltpu.VMEM(positions.shape, F32),
            pltpu.VMEM(probes.shape, F32),
            pltpu.VMEM((4, 8, 128), F32),
            pltpu.VMEM((4, 4, 8, 128), F32),
            pltpu.VMEM((4, 2, 16, 128), F32),
            pltpu.VMEM((4, 128, 16), F32),
            pltpu.VMEM((4, 256, 1536), BF16),
            pltpu.VMEM((4, 256, 1536), BF16),
            pltpu.VMEM((DEG - 1, 4, 2, 16, 128), F32),
            pltpu.VMEM((4, 8, 128), F32),
            pltpu.VMEM((4, 8, 128), F32),
            DMA((2,)),
            DMA((4,)),
            DMA((4,)),
            DMA((4,)),
            DMA((4,)),
            DMA((DEG - 1, 4, 2)),
            DMA((DEG - 1, 4, 2)),
            DMA((4,)),
            DMA((4,)),
        ],
        compiler_params=pltpu.CompilerParams(
            collective_id=0, has_side_effects=True, vmem_limit_bytes=32 * 1024 * 1024
        ),
        name="fused",
    )(*[pltpu.with_memory_space_constraint(x, pltpu.HBM) for x in (positions, probes)])


def block_width(length):
    width = min(length, 512)
    while length % width != 0:
        width = width - 1
    return width


def mobility_block(rows_pos, rows_ids, cols_pos, cols_ids):
    delta = rows_pos[:, :, None] - cols_pos[:, None, :]
    dist_sq = jnp.sum(delta * delta, axis=0)
    same = rows_ids[:, None] == cols_ids[None, :]
    inverse = lax.rsqrt(dist_sq + same.astype(jnp.float32))
    inv_sq = inverse * inverse
    scaled = 0.75 * RADIUS * inverse
    along = jnp.where(same, jnp.float32(1.0), scaled * (1.0 + 2.0 / 3.0 * RADIUS * RADIUS * inv_sq))
    across = jnp.where(
        same, jnp.float32(0.0), scaled * inv_sq * (1.0 - 2.0 * RADIUS * RADIUS * inv_sq)
    )
    identity = jnp.eye(3, dtype=jnp.float32)
    return (
        identity[:, :, None, None] * along[None, None]
        + delta[:, None] * (across[None] * delta)[None]
    )


def gathered(positions, probes):
    seg_len = positions.shape[1]
    probe_count = probes.shape[1]
    n_row = lax.axis_size("row")
    n_col = lax.axis_size("col")
    beads_all = seg_len * n_row * n_col
    places = lax.all_gather(positions, ("row", "col"), axis=1, tiled=True)
    all_ids = jnp.arange(beads_all, dtype=jnp.int32)
    own_at = (lax.axis_index("row") * n_col + lax.axis_index("col")) * seg_len
    own_ids = own_at + jnp.arange(seg_len, dtype=jnp.int32)
    width = block_width(beads_all)

    def apply_mobility(vectors):
        whole = lax.all_gather(vectors, ("row", "col"), axis=2, tiled=True)

        def add_block(block_step, carried):
            offset = block_step * width
            cols_pos = lax.dynamic_slice_in_dim(places, offset, width, 1)
            cols_ids = lax.dynamic_slice_in_dim(all_ids, offset, width, 0)
            mobility = mobility_block(positions, own_ids, cols_pos, cols_ids)
            columns = lax.dynamic_slice_in_dim(whole, offset, width, 2)
            image = carried[0] + jnp.einsum(
                "abrc,bpc->apr", mobility, columns, precision=lax.Precision.HIGHEST
            )
            return image, carried[1] + jnp.sum(jnp.abs(mobility), axis=(1, 3))

        zeros = (jnp.zeros((3, probe_count, seg_len), F32), jnp.zeros((3, seg_len), F32))
        return lax.fori_loop(0, beads_all // width, add_block, zeros)

    image, row_sums = apply_mobility(probes)
    ceiling = lax.pmax(jnp.max(row_sums), ("row", "col"))
    factor = 2.0 / ceiling
    previous = probes
    current = factor * image - probes
    noise_sum = cheb_weight(0) * previous + cheb_weight(1) * current
    for degree_step in range(2, DEG + 1):
        following = 2.0 * (factor * apply_mobility(current)[0] - current) - previous
        previous, current = (current, following)
        noise_sum = noise_sum + cheb_weight(degree_step) * current
    return jnp.sqrt(ceiling) * noise_sum


def solution(mesh):
    split_by = ("groups", "row", "col")
    square = mesh.shape["row"] == 4 and mesh.shape["col"] == 4

    def per_device(positions, probes):
        if square and probes.shape == (3, 16, 64):
            return fused(positions, probes)
        return gathered(positions, probes)

    return jax.shard_map(
        per_device,
        mesh=mesh,
        in_specs=(P(None, split_by), P(None, None, split_by)),
        out_specs=P(None, None, split_by),
        check_vma=False,
    )
```

```python
import functools
import math

import jax
import jax.numpy as jnp
from jax import lax
from jax.experimental import pallas as pl
from jax.experimental.pallas import tpu as pltpu
from jax.sharding import PartitionSpec as P

DEG = 4
RADIUS = 0.3
MESH = pl.DeviceIdType.MESH
F32 = jnp.float32
BF16 = jnp.bfloat16


def cheb_weight(degree_step):
    if degree_step == 0:
        return 2.0 / math.pi
    return 4.0 * (-1.0) ** (degree_step + 1) / (math.pi * (4.0 * degree_step * degree_step - 1.0))


def flip(index, bits):
    for bit in (1, 2, 4, 8):
        if bits & bit:
            index = index + bit - 2 * bit * lax.rem(lax.div(index, bit), 2)
    return index


def split(value):
    high = value.astype(BF16)
    return high, (value - high.astype(F32)).astype(BF16)


def kernel(
    pos_hbm, probes_hbm, out_ref,
    pos_ref, probes_ref, msg, first, field, posT, w_high, w_low, gather, last_out, last_in,
    load, first_send, first_recv, gather_send, gather_recv, last_send, last_recv,
):
    row = lax.axis_index("row")
    col = lax.axis_index("col")
    partners = [(dr, dc) for dc in range(4) for dr in (2, 3, 1, 0) if (dr, dc) != (0, 0)]

    loads = [
        pltpu.make_async_copy(pos_hbm, pos_ref, load.at[0]),
        pltpu.make_async_copy(probes_hbm, probes_ref, load.at[1]),
    ]
    for copy in loads:
        copy.start()
    barrier = pltpu.get_barrier_semaphore()
    for dr, dc in partners:
        pl.semaphore_signal(
            barrier, inc=1, device_id={"row": flip(row, dr), "col": flip(col, dc)}, device_id_type=MESH
        )
    for copy in loads:
        copy.wait()

    scaled_pos = pos_ref[...] * (1.0 / (0.75 * RADIUS))
    for r in range(4):
        mine = [probes_ref[t, 4 * r : 4 * r + 4, :] for t in range(3)]
        left = jnp.concatenate([mine[0], mine[1]], axis=0)
        right = jnp.concatenate([mine[2], scaled_pos, jnp.zeros((1, 64), F32)], axis=0)
        msg[r] = jnp.concatenate([left, right], axis=1)
    first[0, 0] = msg[row]

    pl.semaphore_wait(barrier, len(partners))
    first_copies = {}
    for dr, dc in partners:
        to_row = flip(row, dr)
        copy = pltpu.make_async_remote_copy(
            src_ref=msg.at[to_row],
            dst_ref=first.at[dc, dr],
            send_sem=first_send.at[dc, dr],
            recv_sem=first_recv.at[dc, dr],
            device_id={"row": to_row, "col": flip(col, dc)},
            device_id_type=MESH,
        )
        copy.start()
        first_copies[dc, dr] = copy

    low_lanes = lax.broadcasted_iota(jnp.int32, (8, 128), 1) < 64

    def unpack(dc):
        for h in range(2):
            even, odd = first[dc, 2 * h], first[dc, 2 * h + 1]
            lanes = slice(128 * h, 128 * h + 128)
            field[dc, 0:8, lanes] = jnp.where(low_lanes, even, pltpu.roll(odd, 64, 1))
            field[dc, 8:16, lanes] = jnp.where(low_lanes, pltpu.roll(even, 64, 1), odd)
        pair = jnp.concatenate([field[dc, 8:16, 0:128], field[dc, 8:16, 128:256]], axis=0)
        posT[dc] = pair.T

    unit = (0.75 * RADIUS) ** 2
    c_along = 2.0 / 3.0 * RADIUS * RADIUS / unit
    c_across = 2.0 * RADIUS * RADIUS / unit
    STEP = 16
    own_bead = lax.broadcasted_iota(jnp.int32, (STEP, 128), 1)
    step_bead = lax.broadcasted_iota(jnp.int32, (STEP, 128), 0)
    sums = [[jnp.zeros((8, 128), F32) for _ in range(3)] for _ in range(2)]

    def generate(dc, h):
        for at in range(0, 128, STEP):
            rows = slice(256 * dc + 128 * h + at, 256 * dc + 128 * h + at + STEP)
            centres = [posT[dc, at : at + STEP, 8 * h + 4 + t : 8 * h + 5 + t] for t in range(3)]
            centres = [jnp.broadcast_to(c, (STEP, 128)) for c in centres]
            for own in range(2):
                d = [field[0, 12 + t : 13 + t, 128 * own : 128 * own + 128] - centres[t] for t in range(3)]
                dist_sq = d[0] * d[0] + d[1] * d[1] + d[2] * d[2]
                diagonal = dc == 0 and own == h
                if diagonal:
                    same = (step_bead + at) == own_bead
                    dist_sq = jnp.where(same, 1.0, dist_sq)
                inverse = lax.rsqrt(dist_sq)
                inv_sq = inverse * inverse
                cubed = inverse * inv_sq
                along = inverse + c_along * cubed
                across = cubed - c_across * (cubed * inv_sq)
                if diagonal:
                    along = jnp.where(same, 1.0, along)
                    across = jnp.where(same, 0.0, across)
                g = [across * d[t] for t in range(3)]
                parts = [
                    along + g[0] * d[0], along + g[1] * d[1], along + g[2] * d[2],
                    g[0] * d[1], g[0] * d[2], g[1] * d[2],
                ]
                for k, part in enumerate(parts):
                    high, low = split(part)
                    lanes = slice(768 * own + 128 * k, 768 * own + 128 * k + 128)
                    w_high[rows, lanes] = high
                    w_low[rows, lanes] = low
                mags = [jnp.abs(part) for part in parts]
                mags = [mag[0:8] + mag[8:16] for mag in mags]
                for t, (p, q, r) in enumerate(((0, 3, 4), (1, 3, 5), (2, 4, 5))):
                    sums[own][t] = sums[own][t] + (mags[p] + mags[q] + mags[r])

    def multiply(blocks, dc):
        rows = slice(256 * dc, 256 * (dc + len(blocks)))
        high, low = split(jnp.concatenate(blocks, axis=1))
        both = jnp.concatenate([high, low], axis=0)
        image = jnp.dot(both, w_high[rows], preferred_element_type=F32)
        rest = jnp.dot(high, w_low[rows], preferred_element_type=F32)
        return image[0:16] + image[16:32] + rest

    def combine(acc):
        halves = []
        for own in range(2):
            xx, yy, zz, xy, xz, yz = [
                acc[:, 768 * own + 128 * k : 768 * own + 128 * k + 128] for k in range(6)
            ]
            halves.append(
                jnp.concatenate(
                    [
                        xx[0:4] + xy[4:8] + xz[8:12],
                        xy[0:4] + yy[4:8] + yz[8:12],
                        xz[0:4] + yz[4:8] + zz[8:12],
                    ],
                    axis=0,
                )
            )
        return jnp.concatenate(halves, axis=1)

    def send(k, value):
        gather[k, 0] = value
        copies = {}
        for dc in (3, 2, 1):
            copy = pltpu.make_async_remote_copy(
                src_ref=gather.at[k, 0],
                dst_ref=gather.at[k, dc],
                send_sem=gather_send.at[k, dc],
                recv_sem=gather_recv.at[k, dc],
                device_id={"row": row, "col": flip(col, dc)},
                device_id_type=MESH,
            )
            copy.start()
            copies[dc] = copy
        return copies

    def apply(k, copies):
        acc = multiply([gather[k, 0]], 0)
        for dc in range(1, 4):
            copies[dc].wait_recv()
        return combine(acc + multiply([gather[k, dc] for dc in range(1, 4)], 1))

    for dr in (2, 3, 1):
        first_copies[0, dr].wait_recv()
    unpack(0)
    generate(0, 0)
    generate(0, 1)
    for dc in range(1, 4):
        for dr in range(4):
            first_copies[dc, dr].wait_recv()
    for dc in range(1, 4):
        unpack(dc)
    acc = None
    for dc in range(1, 4):
        generate(dc, 0)
        term = multiply([field[dc - 1]], dc - 1)
        acc = term if acc is None else acc + term
        generate(dc, 1)
    acc = acc + multiply([field[3]], 3)
    image1 = combine(acc)
    row_max = functools.reduce(jnp.maximum, [jnp.sum(s, axis=0, keepdims=True) for half in sums for s in half])
    row_max = jnp.max(row_max, axis=1, keepdims=True)
    copies1 = send(0, jnp.concatenate([image1, jnp.broadcast_to(row_max, (4, 256))], axis=0))
    image2 = apply(0, copies1)
    top = functools.reduce(jnp.maximum, [gather[0, dc, 12:13, :] for dc in range(4)])
    factor = 2.0 / top
    start = field[0, 0:12, :]
    basis1 = factor * image1 - start
    basis2 = 2.0 * (factor * (factor * image2 - image1) - basis1) - start
    pad = jnp.zeros((4, 256), F32)
    copies2 = send(1, jnp.concatenate([basis2, pad], axis=0))
    basis3 = 2.0 * (factor * apply(1, copies2) - basis2) - basis1
    copies3 = send(2, jnp.concatenate([basis3, pad], axis=0))
    noise = cheb_weight(0) * start + cheb_weight(1) * basis1
    noise = noise + cheb_weight(2) * basis2 + cheb_weight(3) * basis3
    basis4 = 2.0 * (factor * apply(2, copies3) - basis3) - basis2
    noise = jnp.sqrt(top) * (noise + cheb_weight(4) * basis4)

    noise = jnp.concatenate([noise, pad], axis=0)
    last_copies = []
    for dr in (2, 3, 1, 0):
        h = dr // 2
        upper = noise[0:8, 128 * h : 128 * h + 128]
        lower = noise[8:16, 128 * h : 128 * h + 128]
        if dr % 2 == 0:
            tile = jnp.where(low_lanes, upper, pltpu.roll(lower, 64, 1))
        else:
            tile = jnp.where(low_lanes, pltpu.roll(upper, 64, 1), lower)
        if dr == 0:
            last_in[row] = tile
        else:
            last_out[dr] = tile
            copy = pltpu.make_async_remote_copy(
                src_ref=last_out.at[dr],
                dst_ref=last_in.at[row],
                send_sem=last_send.at[dr],
                recv_sem=last_recv.at[dr],
                device_id={"row": flip(row, dr), "col": col},
                device_id_type=MESH,
            )
            copy.start()
            last_copies.append(copy)
    for copy in list(first_copies.values()):
        copy.wait_send()
    for copies in (copies1, copies2, copies3):
        for copy in copies.values():
            copy.wait_send()
    for copy in last_copies:
        copy.wait()
    for q in range(4):
        tile = last_in[q]
        out_ref[0, 4 * q : 4 * q + 4, :] = tile[0:4, 0:64]
        out_ref[1, 4 * q : 4 * q + 4, :] = tile[4:8, 0:64]
        out_ref[2, 4 * q : 4 * q + 4, :] = tile[0:4, 64:128]


def fused(positions, probes):
    DMA = pltpu.SemaphoreType.DMA
    return pl.pallas_call(
        kernel,
        out_shape=jax.ShapeDtypeStruct(probes.shape, F32),
        in_specs=[pl.BlockSpec(memory_space=pltpu.HBM)] * 2,
        out_specs=pl.BlockSpec(memory_space=pltpu.VMEM),
        scratch_shapes=[
            pltpu.VMEM(positions.shape, F32),
            pltpu.VMEM(probes.shape, F32),
            pltpu.VMEM((4, 8, 128), F32),
            pltpu.VMEM((4, 4, 8, 128), F32),
            pltpu.VMEM((4, 16, 256), F32),
            pltpu.VMEM((4, 128, 16), F32),
            pltpu.VMEM((1024, 1536), BF16),
            pltpu.VMEM((1024, 1536), BF16),
            pltpu.VMEM((DEG - 1, 4, 16, 256), F32),
            pltpu.VMEM((4, 8, 128), F32),
            pltpu.VMEM((4, 8, 128), F32),
            DMA((2,)),
            DMA((4, 4)),
            DMA((4, 4)),
            DMA((DEG - 1, 4)),
            DMA((DEG - 1, 4)),
            DMA((4,)),
            DMA((4,)),
        ],
        compiler_params=pltpu.CompilerParams(
            collective_id=0, has_side_effects=True, vmem_limit_bytes=32 * 1024 * 1024
        ),
        name="fused",
    )(*[pltpu.with_memory_space_constraint(x, pltpu.HBM) for x in (positions, probes)])


def block_width(length):
    width = min(length, 512)
    while length % width != 0:
        width = width - 1
    return width


def mobility_block(rows_pos, rows_ids, cols_pos, cols_ids):
    delta = rows_pos[:, :, None] - cols_pos[:, None, :]
    dist_sq = jnp.sum(delta * delta, axis=0)
    same = rows_ids[:, None] == cols_ids[None, :]
    inverse = lax.rsqrt(dist_sq + same.astype(jnp.float32))
    inv_sq = inverse * inverse
    scaled = 0.75 * RADIUS * inverse
    along = jnp.where(same, jnp.float32(1.0), scaled * (1.0 + 2.0 / 3.0 * RADIUS * RADIUS * inv_sq))
    across = jnp.where(
        same, jnp.float32(0.0), scaled * inv_sq * (1.0 - 2.0 * RADIUS * RADIUS * inv_sq)
    )
    identity = jnp.eye(3, dtype=jnp.float32)
    return (
        identity[:, :, None, None] * along[None, None]
        + delta[:, None] * (across[None] * delta)[None]
    )


def gathered(positions, probes):
    seg_len = positions.shape[1]
    probe_count = probes.shape[1]
    n_row = lax.axis_size("row")
    n_col = lax.axis_size("col")
    beads_all = seg_len * n_row * n_col
    places = lax.all_gather(positions, ("row", "col"), axis=1, tiled=True)
    all_ids = jnp.arange(beads_all, dtype=jnp.int32)
    own_at = (lax.axis_index("row") * n_col + lax.axis_index("col")) * seg_len
    own_ids = own_at + jnp.arange(seg_len, dtype=jnp.int32)
    width = block_width(beads_all)

    def apply_mobility(vectors):
        whole = lax.all_gather(vectors, ("row", "col"), axis=2, tiled=True)

        def add_block(block_step, carried):
            offset = block_step * width
            cols_pos = lax.dynamic_slice_in_dim(places, offset, width, 1)
            cols_ids = lax.dynamic_slice_in_dim(all_ids, offset, width, 0)
            mobility = mobility_block(positions, own_ids, cols_pos, cols_ids)
            columns = lax.dynamic_slice_in_dim(whole, offset, width, 2)
            image = carried[0] + jnp.einsum(
                "abrc,bpc->apr", mobility, columns, precision=lax.Precision.HIGHEST
            )
            return image, carried[1] + jnp.sum(jnp.abs(mobility), axis=(1, 3))

        zeros = (jnp.zeros((3, probe_count, seg_len), F32), jnp.zeros((3, seg_len), F32))
        return lax.fori_loop(0, beads_all // width, add_block, zeros)

    image, row_sums = apply_mobility(probes)
    ceiling = lax.pmax(jnp.max(row_sums), ("row", "col"))
    factor = 2.0 / ceiling
    previous = probes
    current = factor * image - probes
    noise_sum = cheb_weight(0) * previous + cheb_weight(1) * current
    for degree_step in range(2, DEG + 1):
        following = 2.0 * (factor * apply_mobility(current)[0] - current) - previous
        previous, current = (current, following)
        noise_sum = noise_sum + cheb_weight(degree_step) * current
    return jnp.sqrt(ceiling) * noise_sum


def solution(mesh):
    split_by = ("groups", "row", "col")
    square = mesh.shape["row"] == 4 and mesh.shape["col"] == 4

    def per_device(positions, probes):
        if square and probes.shape == (3, 16, 64):
            return fused(positions, probes)
        return gathered(positions, probes)

    return jax.shard_map(
        per_device,
        mesh=mesh,
        in_specs=(P(None, split_by), P(None, None, split_by)),
        out_specs=P(None, None, split_by),
        check_vma=False,
    )
```

```python
import functools
import math

import jax
import jax.numpy as jnp
from jax import lax
from jax.experimental import pallas as pl
from jax.experimental.pallas import tpu as pltpu
from jax.sharding import PartitionSpec as P

DEG = 4
RADIUS = 0.3
MESH = pl.DeviceIdType.MESH
F32 = jnp.float32
BF16 = jnp.bfloat16


def cheb_weight(degree_step):
    if degree_step == 0:
        return 2.0 / math.pi
    return 4.0 * (-1.0) ** (degree_step + 1) / (math.pi * (4.0 * degree_step * degree_step - 1.0))


def flip(index, bits):
    for bit in (1, 2, 4, 8):
        if bits & bit:
            index = index + bit - 2 * bit * lax.rem(lax.div(index, bit), 2)
    return index


def split(value):
    high = value.astype(BF16)
    return high, (value - high.astype(F32)).astype(BF16)


def kernel(
    pos_hbm, probes_hbm, out_ref,
    pos_ref, probes_ref, msg, first, field, posT, w_high, w_low, gather, states, last_out, last_in,
    load, first_send, first_recv, gather_send, gather_recv, last_send, last_recv,
):
    row = lax.axis_index("row")
    col = lax.axis_index("col")
    partners = [(dr, dc) for dc in range(4) for dr in (2, 3, 1, 0) if (dr, dc) != (0, 0)]

    loads = [
        pltpu.make_async_copy(pos_hbm, pos_ref, load.at[0]),
        pltpu.make_async_copy(probes_hbm, probes_ref, load.at[1]),
    ]
    for copy in loads:
        copy.start()
    barrier = pltpu.get_barrier_semaphore()
    for dr, dc in partners:
        pl.semaphore_signal(
            barrier, inc=1, device_id={"row": flip(row, dr), "col": flip(col, dc)}, device_id_type=MESH
        )
    for copy in loads:
        copy.wait()

    scaled_pos = pos_ref[...] * (1.0 / (0.75 * RADIUS))
    for r in range(4):
        mine = [probes_ref[t, 4 * r : 4 * r + 4, :] for t in range(3)]
        left = jnp.concatenate([mine[0], mine[1]], axis=0)
        right = jnp.concatenate([mine[2], scaled_pos, jnp.ones((1, 64), F32)], axis=0)
        msg[r] = jnp.concatenate([left, right], axis=1)
    first[0, 0] = msg[row]

    pl.semaphore_wait(barrier, len(partners))
    first_copies = {}
    for dr, dc in partners:
        to_row = flip(row, dr)
        copy = pltpu.make_async_remote_copy(
            src_ref=msg.at[to_row],
            dst_ref=first.at[dc, dr],
            send_sem=first_send.at[dc, dr],
            recv_sem=first_recv.at[dc, dr],
            device_id={"row": to_row, "col": flip(col, dc)},
            device_id_type=MESH,
        )
        copy.start()
        first_copies[dc, dr] = copy

    low_lanes = lax.broadcasted_iota(jnp.int32, (8, 128), 1) < 64

    def unpack(dc):
        for h in range(2):
            even, odd = first[dc, 2 * h], first[dc, 2 * h + 1]
            lanes = slice(128 * h, 128 * h + 128)
            field[dc, 0:8, lanes] = jnp.where(low_lanes, even, pltpu.roll(odd, 64, 1))
            field[dc, 8:16, lanes] = jnp.where(low_lanes, pltpu.roll(even, 64, 1), odd)
        pair = jnp.concatenate([field[dc, 8:16, 0:128], field[dc, 8:16, 128:256]], axis=0)
        posT[dc] = pair.T

    unit = (0.75 * RADIUS) ** 2
    c_along = 2.0 / 3.0 * RADIUS * RADIUS / unit
    c_across = 2.0 * RADIUS * RADIUS / unit
    STEP = 16
    own_bead = lax.broadcasted_iota(jnp.int32, (STEP, 128), 1)
    step_bead = lax.broadcasted_iota(jnp.int32, (STEP, 128), 0)

    def generate(dc, h, sums):
        sums = [list(half) for half in sums]
        for at in range(0, 128, STEP):
            rows = pl.ds(pl.multiple_of(256 * dc + 128 * h + at, STEP), STEP)
            centres = posT[dc, at : at + STEP, :]
            centres = [centres[:, 8 * h + 4 + t : 8 * h + 5 + t] for t in range(3)]
            centres = [jnp.broadcast_to(c, (STEP, 128)) for c in centres]
            for own in range(2):
                d = [field[0, 12 + t : 13 + t, 128 * own : 128 * own + 128] - centres[t] for t in range(3)]
                dist_sq = d[0] * d[0] + d[1] * d[1] + d[2] * d[2]
                diagonal = isinstance(dc, int) and dc == 0 and own == h
                if diagonal:
                    same = (step_bead + at) == own_bead
                    dist_sq = jnp.where(same, 1.0, dist_sq)
                inverse = lax.rsqrt(dist_sq)
                inv_sq = inverse * inverse
                cubed = inverse * inv_sq
                along = inverse + c_along * cubed
                across = cubed - c_across * (cubed * inv_sq)
                if diagonal:
                    along = jnp.where(same, 1.0, along)
                    across = jnp.where(same, 0.0, across)
                g = [across * d[t] for t in range(3)]
                parts = [
                    along + g[0] * d[0], along + g[1] * d[1], along + g[2] * d[2],
                    g[0] * d[1], g[0] * d[2], g[1] * d[2],
                ]
                for k, part in enumerate(parts):
                    high, low = split(part)
                    lanes = slice(768 * own + 128 * k, 768 * own + 128 * k + 128)
                    w_high[rows, lanes] = high
                    w_low[rows, lanes] = low
                for t in range(3):
                    mag = jnp.abs(parts[3 + t])
                    sums[own][t] = sums[own][t] + (mag[0:8] + mag[8:16])
        return tuple(tuple(half) for half in sums)

    def multiply(block, dc):
        rows = pl.ds(pl.multiple_of(256 * dc, 256), 256)
        high, low = split(block)
        both = jnp.concatenate([high, low], axis=0)
        image = jnp.dot(both, w_high[rows, :], preferred_element_type=F32)
        rest = jnp.dot(high, w_low[rows, :], preferred_element_type=F32)
        return image[0:16] + image[16:32] + rest

    def combine(acc):
        halves = []
        for own in range(2):
            xx, yy, zz, xy, xz, yz = [
                acc[:, 768 * own + 128 * k : 768 * own + 128 * k + 128] for k in range(6)
            ]
            halves.append(
                jnp.concatenate(
                    [
                        xx[0:4] + xy[4:8] + xz[8:12],
                        xy[0:4] + yy[4:8] + yz[8:12],
                        xz[0:4] + yz[4:8] + zz[8:12],
                    ],
                    axis=0,
                )
            )
        return jnp.concatenate(halves, axis=1)

    def gather_copy(k, dc, to_col):
        return pltpu.make_async_remote_copy(
            src_ref=gather.at[k, 0],
            dst_ref=gather.at[k, dc],
            send_sem=gather_send.at[k, dc],
            recv_sem=gather_recv.at[k, dc],
            device_id={"row": row, "col": to_col},
            device_id_type=MESH,
        )

    def send(k, value):
        gather[k, 0] = value
        for dc in (3, 2, 1):
            gather_copy(k, dc, flip(col, dc)).start()

    for dr in (2, 3, 1):
        first_copies[0, dr].wait_recv()
    unpack(0)
    sums = tuple(tuple(jnp.zeros((8, 128), F32) for _ in range(3)) for _ in range(2))
    sums = generate(0, 0, sums)
    sums = generate(0, 1, sums)
    for dc in range(1, 4):
        for dr in range(4):
            first_copies[dc, dr].wait_recv()
    for dc in range(1, 4):
        unpack(dc)

    def grow(dc, carried):
        acc, sums = carried
        sums = generate(dc, 0, sums)
        acc = acc + multiply(field[dc - 1], dc - 1)
        return acc, generate(dc, 1, sums)

    acc, sums = lax.fori_loop(1, 4, grow, (jnp.zeros((16, 1536), F32), sums))
    acc = acc + multiply(field[3], 3)
    image1 = combine(acc)
    row_max = None
    for own in range(2):
        xx, yy, zz = [acc[15:16, 768 * own + 128 * k : 768 * own + 128 * k + 128] for k in range(3)]
        xy, xz, yz = [jnp.sum(s, axis=0, keepdims=True) for s in sums[own]]
        largest = jnp.maximum(jnp.maximum(xx + xy + xz, xy + yy + yz), xz + yz + zz)
        row_max = largest if row_max is None else jnp.maximum(row_max, largest)
    row_max = jnp.max(row_max, axis=1, keepdims=True)
    send(0, jnp.concatenate([image1, jnp.broadcast_to(row_max, (4, 256))], axis=0))

    pad = jnp.zeros((4, 256), F32)
    states[0, 0:12] = field[0, 0:12, :]
    states[1, 0:12] = image1

    def degree(k, carried):
        def block(dc, acc):
            @pl.when(dc > 0)
            def _():
                gather_copy(k, dc, flip(col, 1)).wait_recv()

            return acc + multiply(gather[k, dc], dc)

        image = combine(lax.fori_loop(0, 4, block, jnp.zeros((16, 1536), F32)))
        top = functools.reduce(jnp.maximum, [gather[0, dc, 12:13, :] for dc in range(4)])
        factor = 2.0 / top
        older, last = states[0, 0:12], states[1, 0:12]
        opening = k == 0
        last1 = jnp.where(opening, factor * last - older, last)
        image = factor * jnp.where(opening, factor * image - last, image)
        following = 2.0 * (image - last1) - older
        total = jnp.where(opening, cheb_weight(0) * older + cheb_weight(1) * last1, states[2, 0:12])
        weight = jnp.where(opening, cheb_weight(2), jnp.where(k == 1, cheb_weight(3), cheb_weight(4)))
        states[2, 0:12] = total + weight * following
        states[0, 0:12] = last1
        states[1, 0:12] = following

        @pl.when(k < DEG - 2)
        def _():
            send(k + 1, jnp.concatenate([following, pad], axis=0))

        return carried

    lax.fori_loop(0, DEG - 1, degree, 0)
    top = functools.reduce(jnp.maximum, [gather[0, dc, 12:13, :] for dc in range(4)])
    noise = jnp.sqrt(top) * states[2, 0:12]

    noise = jnp.concatenate([noise, pad], axis=0)
    last_copies = []
    for dr in (2, 3, 1, 0):
        h = dr // 2
        upper = noise[0:8, 128 * h : 128 * h + 128]
        lower = noise[8:16, 128 * h : 128 * h + 128]
        if dr % 2 == 0:
            tile = jnp.where(low_lanes, upper, pltpu.roll(lower, 64, 1))
        else:
            tile = jnp.where(low_lanes, pltpu.roll(upper, 64, 1), lower)
        if dr == 0:
            last_in[row] = tile
        else:
            last_out[dr] = tile
            copy = pltpu.make_async_remote_copy(
                src_ref=last_out.at[dr],
                dst_ref=last_in.at[row],
                send_sem=last_send.at[dr],
                recv_sem=last_recv.at[dr],
                device_id={"row": flip(row, dr), "col": col},
                device_id_type=MESH,
            )
            copy.start()
            last_copies.append(copy)
    for copy in list(first_copies.values()):
        copy.wait_send()
    for k in range(DEG - 1):
        for dc in (3, 2, 1):
            gather_copy(k, dc, flip(col, dc)).wait_send()
    for copy in last_copies:
        copy.wait()
    for q in range(4):
        tile = last_in[q]
        out_ref[0, 4 * q : 4 * q + 4, :] = tile[0:4, 0:64]
        out_ref[1, 4 * q : 4 * q + 4, :] = tile[4:8, 0:64]
        out_ref[2, 4 * q : 4 * q + 4, :] = tile[0:4, 64:128]


def fused(positions, probes):
    DMA = pltpu.SemaphoreType.DMA
    return pl.pallas_call(
        kernel,
        out_shape=jax.ShapeDtypeStruct(probes.shape, F32),
        in_specs=[pl.BlockSpec(memory_space=pltpu.HBM)] * 2,
        out_specs=pl.BlockSpec(memory_space=pltpu.VMEM),
        scratch_shapes=[
            pltpu.VMEM(positions.shape, F32),
            pltpu.VMEM(probes.shape, F32),
            pltpu.VMEM((4, 8, 128), F32),
            pltpu.VMEM((4, 4, 8, 128), F32),
            pltpu.VMEM((4, 16, 256), F32),
            pltpu.VMEM((4, 128, 16), F32),
            pltpu.VMEM((1024, 1536), BF16),
            pltpu.VMEM((1024, 1536), BF16),
            pltpu.VMEM((DEG - 1, 4, 16, 256), F32),
            pltpu.VMEM((3, 16, 256), F32),
            pltpu.VMEM((4, 8, 128), F32),
            pltpu.VMEM((4, 8, 128), F32),
            DMA((2,)),
            DMA((4, 4)),
            DMA((4, 4)),
            DMA((DEG - 1, 4)),
            DMA((DEG - 1, 4)),
            DMA((4,)),
            DMA((4,)),
        ],
        compiler_params=pltpu.CompilerParams(
            collective_id=0, has_side_effects=True, vmem_limit_bytes=32 * 1024 * 1024
        ),
        name="fused",
    )(*[pltpu.with_memory_space_constraint(x, pltpu.HBM) for x in (positions, probes)])


def block_width(length):
    width = min(length, 512)
    while length % width != 0:
        width = width - 1
    return width


def mobility_block(rows_pos, rows_ids, cols_pos, cols_ids):
    delta = rows_pos[:, :, None] - cols_pos[:, None, :]
    dist_sq = jnp.sum(delta * delta, axis=0)
    same = rows_ids[:, None] == cols_ids[None, :]
    inverse = lax.rsqrt(dist_sq + same.astype(jnp.float32))
    inv_sq = inverse * inverse
    scaled = 0.75 * RADIUS * inverse
    along = jnp.where(same, jnp.float32(1.0), scaled * (1.0 + 2.0 / 3.0 * RADIUS * RADIUS * inv_sq))
    across = jnp.where(
        same, jnp.float32(0.0), scaled * inv_sq * (1.0 - 2.0 * RADIUS * RADIUS * inv_sq)
    )
    identity = jnp.eye(3, dtype=jnp.float32)
    return (
        identity[:, :, None, None] * along[None, None]
        + delta[:, None] * (across[None] * delta)[None]
    )


def gathered(positions, probes):
    seg_len = positions.shape[1]
    probe_count = probes.shape[1]
    n_row = lax.axis_size("row")
    n_col = lax.axis_size("col")
    beads_all = seg_len * n_row * n_col
    places = lax.all_gather(positions, ("row", "col"), axis=1, tiled=True)
    all_ids = jnp.arange(beads_all, dtype=jnp.int32)
    own_at = (lax.axis_index("row") * n_col + lax.axis_index("col")) * seg_len
    own_ids = own_at + jnp.arange(seg_len, dtype=jnp.int32)
    width = block_width(beads_all)

    def apply_mobility(vectors):
        whole = lax.all_gather(vectors, ("row", "col"), axis=2, tiled=True)

        def add_block(block_step, carried):
            offset = block_step * width
            cols_pos = lax.dynamic_slice_in_dim(places, offset, width, 1)
            cols_ids = lax.dynamic_slice_in_dim(all_ids, offset, width, 0)
            mobility = mobility_block(positions, own_ids, cols_pos, cols_ids)
            columns = lax.dynamic_slice_in_dim(whole, offset, width, 2)
            image = carried[0] + jnp.einsum(
                "abrc,bpc->apr", mobility, columns, precision=lax.Precision.HIGHEST
            )
            return image, carried[1] + jnp.sum(jnp.abs(mobility), axis=(1, 3))

        zeros = (jnp.zeros((3, probe_count, seg_len), F32), jnp.zeros((3, seg_len), F32))
        return lax.fori_loop(0, beads_all // width, add_block, zeros)

    image, row_sums = apply_mobility(probes)
    ceiling = lax.pmax(jnp.max(row_sums), ("row", "col"))
    factor = 2.0 / ceiling
    previous = probes
    current = factor * image - probes
    noise_sum = cheb_weight(0) * previous + cheb_weight(1) * current
    for degree_step in range(2, DEG + 1):
        following = 2.0 * (factor * apply_mobility(current)[0] - current) - previous
        previous, current = (current, following)
        noise_sum = noise_sum + cheb_weight(degree_step) * current
    return jnp.sqrt(ceiling) * noise_sum


def solution(mesh):
    split_by = ("groups", "row", "col")
    square = mesh.shape["row"] == 4 and mesh.shape["col"] == 4

    def per_device(positions, probes):
        if square and probes.shape == (3, 16, 64):
            return fused(positions, probes)
        return gathered(positions, probes)

    return jax.shard_map(
        per_device,
        mesh=mesh,
        in_specs=(P(None, split_by), P(None, None, split_by)),
        out_specs=P(None, None, split_by),
        check_vma=False,
    )
```

```python
import functools
import math

import jax
import jax.numpy as jnp
from jax import lax
from jax.experimental import pallas as pl
from jax.experimental.pallas import tpu as pltpu
from jax.sharding import PartitionSpec as P

DEG = 4
RADIUS = 0.3
MESH = pl.DeviceIdType.MESH
F32 = jnp.float32
BF16 = jnp.bfloat16


def cheb_weight(degree_step):
    if degree_step == 0:
        return 2.0 / math.pi
    return 4.0 * (-1.0) ** (degree_step + 1) / (math.pi * (4.0 * degree_step * degree_step - 1.0))


def flips(index):
    third = 3 - index
    return [index, lax.rem(third + 2, 4), lax.rem(index + 2, 4), third]


def split(value):
    high = value.astype(BF16)
    return high, (value - high.astype(F32)).astype(BF16)


def kernel(
    pos_hbm, probes_hbm, out_ref,
    pos_ref, probes_ref, msg, first, field, posT, w_high, w_low, gather, last_out, last_in,
    load, first_send, first_recv, gather_send, gather_recv, last_send, last_recv,
):
    row = lax.axis_index("row")
    col = lax.axis_index("col")
    rows_by, cols_by = flips(row), flips(col)
    partners = [(dr, dc) for dc in range(4) for dr in (2, 3, 1, 0) if (dr, dc) != (0, 0)]

    loads = [
        pltpu.make_async_copy(pos_hbm, pos_ref, load.at[0]),
        pltpu.make_async_copy(probes_hbm, probes_ref, load.at[1]),
    ]
    barrier = pltpu.get_barrier_semaphore()
    for dr, dc in partners:
        pl.semaphore_signal(
            barrier, inc=1, device_id={"row": rows_by[dr], "col": cols_by[dc]}, device_id_type=MESH
        )
    for copy in loads:
        copy.start()
    for copy in loads:
        copy.wait()

    scaled_pos = pos_ref[...] * (1.0 / (0.75 * RADIUS))
    for r in range(4):
        mine = [probes_ref[t, 4 * r : 4 * r + 4, :] for t in range(3)]
        left = jnp.concatenate([mine[0], mine[1]], axis=0)
        right = jnp.concatenate([mine[2], scaled_pos, jnp.ones((1, 64), F32)], axis=0)
        msg[r] = jnp.concatenate([left, right], axis=1)
    first[0, 0] = msg[row]

    pl.semaphore_wait(barrier, len(partners))
    first_copies = {}
    for dr, dc in partners:
        to_row = rows_by[dr]
        copy = pltpu.make_async_remote_copy(
            src_ref=msg.at[to_row],
            dst_ref=first.at[dc, dr],
            send_sem=first_send.at[dc, dr],
            recv_sem=first_recv.at[dc, dr],
            device_id={"row": to_row, "col": cols_by[dc]},
            device_id_type=MESH,
        )
        copy.start()
        first_copies[dc, dr] = copy

    low_lanes = lax.broadcasted_iota(jnp.int32, (8, 128), 1) < 64

    def unpack(dc):
        for h in range(2):
            even, odd = first[dc, 2 * h], first[dc, 2 * h + 1]
            lanes = slice(128 * h, 128 * h + 128)
            field[dc, 0:8, lanes] = jnp.where(low_lanes, even, pltpu.roll(odd, 64, 1))
            field[dc, 8:16, lanes] = jnp.where(low_lanes, pltpu.roll(even, 64, 1), odd)
        pair = jnp.concatenate([field[dc, 8:16, 0:128], field[dc, 8:16, 128:256]], axis=0)
        posT[dc] = pair.T

    unit = (0.75 * RADIUS) ** 2
    c_along = 2.0 / 3.0 * RADIUS * RADIUS / unit
    c_across = 2.0 * RADIUS * RADIUS / unit
    STEP = 16
    own_bead = lax.broadcasted_iota(jnp.int32, (STEP, 128), 1)
    step_bead = lax.broadcasted_iota(jnp.int32, (STEP, 128), 0)

    def generate(dc, h, sums):
        sums = [list(half) for half in sums]
        for at in range(0, 128, STEP):
            rows = slice(256 * dc + 128 * h + at, 256 * dc + 128 * h + at + STEP)
            centres = posT[dc, at : at + STEP, :]
            centres = [centres[:, 8 * h + 4 + t : 8 * h + 5 + t] for t in range(3)]
            centres = [jnp.broadcast_to(c, (STEP, 128)) for c in centres]
            for own in range(2):
                d = [field[0, 12 + t : 13 + t, 128 * own : 128 * own + 128] - centres[t] for t in range(3)]
                dist_sq = d[0] * d[0] + d[1] * d[1] + d[2] * d[2]
                diagonal = dc == 0 and own == h
                if diagonal:
                    same = (step_bead + at) == own_bead
                    dist_sq = jnp.where(same, 1.0, dist_sq)
                inverse = lax.rsqrt(dist_sq)
                inv_sq = inverse * inverse
                cubed = inverse * inv_sq
                along = inverse + c_along * cubed
                across = cubed - c_across * (cubed * inv_sq)
                if diagonal:
                    along = jnp.where(same, 1.0, along)
                    across = jnp.where(same, 0.0, across)
                g = [across * d[t] for t in range(3)]
                parts = [
                    along + g[0] * d[0], along + g[1] * d[1], along + g[2] * d[2],
                    g[0] * d[1], g[0] * d[2], g[1] * d[2],
                ]
                for k, part in enumerate(parts):
                    high, low = split(part)
                    lanes = slice(768 * own + 128 * k, 768 * own + 128 * k + 128)
                    w_high[rows, lanes] = high
                    w_low[rows, lanes] = low
                for t in range(3):
                    mag = jnp.abs(parts[3 + t])
                    sums[own][t] = sums[own][t] + (mag[0:8] + mag[8:16])
        return tuple(tuple(half) for half in sums)

    def multiply(blocks, dc):
        rows = slice(256 * dc, 256 * (dc + len(blocks)))
        high, low = split(jnp.concatenate(blocks, axis=1))
        both = jnp.concatenate([high, low], axis=0)
        image = jnp.dot(both, w_high[rows, :], preferred_element_type=F32)
        rest = jnp.dot(high, w_low[rows, :], preferred_element_type=F32)
        return image[0:16] + image[16:32] + rest

    def combine(acc):
        packed = []
        at = {"x": (0, 3, 4), "y": (3, 1, 5), "z": (4, 5, 2)}
        for component in "xyz":
            for own in range(2):
                terms = [
                    acc[4 * t : 4 * t + 4, 768 * own + 128 * k : 768 * own + 128 * k + 128]
                    for t, k in enumerate(at[component])
                ]
                packed.append(terms[0] + terms[1] + terms[2])
        return jnp.concatenate(packed, axis=0)

    def pack(block):
        return jnp.concatenate(
            [block[4 * t : 4 * t + 4, 128 * h : 128 * h + 128] for t in range(3) for h in range(2)], axis=0
        )

    def unpacked(packed):
        return jnp.concatenate(
            [
                jnp.concatenate(
                    [packed[8 * t + 4 * h : 8 * t + 4 * h + 4] for t in range(3)] + [jnp.zeros((4, 128), F32)],
                    axis=0,
                )
                for h in range(2)
            ],
            axis=1,
        )

    gather_copies = {}

    def send(k, value):
        rows = slice(0, value.shape[0])
        gather[k, 0, rows] = value
        for dc in (3, 2, 1):
            gather_copies[k, dc] = pltpu.make_async_remote_copy(
                src_ref=gather.at[k, 0, rows],
                dst_ref=gather.at[k, dc, rows],
                send_sem=gather_send.at[k, dc],
                recv_sem=gather_recv.at[k, dc],
                device_id={"row": row, "col": cols_by[dc]},
                device_id_type=MESH,
            )
            gather_copies[k, dc].start()

    def apply(k):
        acc = multiply([unpacked(gather[k, 0, 0:24])], 0)
        for dc in range(1, 4):
            gather_copies[k, dc].wait_recv()
        return combine(acc + multiply([unpacked(gather[k, dc, 0:24]) for dc in range(1, 4)], 1))

    for dr in (2, 3, 1):
        first_copies[0, dr].wait_recv()
    unpack(0)
    sums = tuple(tuple(jnp.zeros((8, 128), F32) for _ in range(3)) for _ in range(2))
    sums = generate(0, 0, sums)
    sums = generate(0, 1, sums)
    for dc in range(1, 4):
        for dr in range(4):
            first_copies[dc, dr].wait_recv()
    for dc in range(1, 4):
        unpack(dc)

    acc = None
    for dc in range(1, 4):
        sums = generate(dc, 0, sums)
        term = multiply([field[dc - 1]], dc - 1)
        acc = term if acc is None else acc + term
        sums = generate(dc, 1, sums)
    acc = acc + multiply([field[3]], 3)
    image1 = combine(acc)
    row_max = None
    for own in range(2):
        xx, yy, zz = [acc[15:16, 768 * own + 128 * k : 768 * own + 128 * k + 128] for k in range(3)]
        xy, xz, yz = [jnp.sum(s, axis=0, keepdims=True) for s in sums[own]]
        largest = jnp.maximum(jnp.maximum(xx + xy + xz, xy + yy + yz), xz + yz + zz)
        row_max = largest if row_max is None else jnp.maximum(row_max, largest)
    row_max = jnp.max(row_max, axis=1, keepdims=True)
    send(0, jnp.concatenate([image1, jnp.broadcast_to(row_max, (8, 128))], axis=0))
    start = pack(field[0])
    image2 = apply(0)
    top = functools.reduce(jnp.maximum, [gather[0, dc, 24:25, :] for dc in range(4)])
    factor = 2.0 / top
    basis1 = factor * image1 - start
    basis2 = 2.0 * (factor * (factor * image2 - image1) - basis1) - start
    send(1, basis2)
    noise = cheb_weight(0) * start + cheb_weight(1) * basis1 + cheb_weight(2) * basis2
    basis3 = 2.0 * (factor * apply(1) - basis2) - basis1
    send(2, basis3)
    noise = noise + cheb_weight(3) * basis3
    basis4 = 2.0 * (factor * apply(2) - basis3) - basis2
    noise = unpacked(jnp.sqrt(top) * (noise + cheb_weight(4) * basis4))

    last_copies = []
    for dr in (2, 3, 1, 0):
        h = dr // 2
        upper = noise[0:8, 128 * h : 128 * h + 128]
        lower = noise[8:16, 128 * h : 128 * h + 128]
        if dr % 2 == 0:
            tile = jnp.where(low_lanes, upper, pltpu.roll(lower, 64, 1))
        else:
            tile = jnp.where(low_lanes, pltpu.roll(upper, 64, 1), lower)
        if dr == 0:
            last_in[row] = tile
        else:
            last_out[dr] = tile
            copy = pltpu.make_async_remote_copy(
                src_ref=last_out.at[dr],
                dst_ref=last_in.at[row],
                send_sem=last_send.at[dr],
                recv_sem=last_recv.at[dr],
                device_id={"row": rows_by[dr], "col": col},
                device_id_type=MESH,
            )
            copy.start()
            last_copies.append(copy)
    for copy in list(first_copies.values()):
        copy.wait_send()
    for copy in gather_copies.values():
        copy.wait_send()
    for copy in last_copies:
        copy.wait()
    for q in range(4):
        tile = last_in[q]
        out_ref[0, 4 * q : 4 * q + 4, :] = tile[0:4, 0:64]
        out_ref[1, 4 * q : 4 * q + 4, :] = tile[4:8, 0:64]
        out_ref[2, 4 * q : 4 * q + 4, :] = tile[0:4, 64:128]


def fused(positions, probes):
    DMA = pltpu.SemaphoreType.DMA
    return pl.pallas_call(
        kernel,
        out_shape=jax.ShapeDtypeStruct(probes.shape, F32),
        in_specs=[pl.BlockSpec(memory_space=pltpu.HBM)] * 2,
        out_specs=pl.BlockSpec(memory_space=pltpu.VMEM),
        scratch_shapes=[
            pltpu.VMEM(positions.shape, F32),
            pltpu.VMEM(probes.shape, F32),
            pltpu.VMEM((4, 8, 128), F32),
            pltpu.VMEM((4, 4, 8, 128), F32),
            pltpu.VMEM((4, 16, 256), F32),
            pltpu.VMEM((4, 128, 16), F32),
            pltpu.VMEM((1024, 1536), BF16),
            pltpu.VMEM((1024, 1536), BF16),
            pltpu.VMEM((DEG - 1, 4, 32, 128), F32),
            pltpu.VMEM((4, 8, 128), F32),
            pltpu.VMEM((4, 8, 128), F32),
            DMA((2,)),
            DMA((4, 4)),
            DMA((4, 4)),
            DMA((DEG - 1, 4)),
            DMA((DEG - 1, 4)),
            DMA((4,)),
            DMA((4,)),
        ],
        compiler_params=pltpu.CompilerParams(
            collective_id=0, has_side_effects=True, vmem_limit_bytes=32 * 1024 * 1024
        ),
        name="fused",
    )(*[pltpu.with_memory_space_constraint(x, pltpu.HBM) for x in (positions, probes)])


def block_width(length):
    width = min(length, 512)
    while length % width != 0:
        width = width - 1
    return width


def mobility_block(rows_pos, rows_ids, cols_pos, cols_ids):
    delta = rows_pos[:, :, None] - cols_pos[:, None, :]
    dist_sq = jnp.sum(delta * delta, axis=0)
    same = rows_ids[:, None] == cols_ids[None, :]
    inverse = lax.rsqrt(dist_sq + same.astype(jnp.float32))
    inv_sq = inverse * inverse
    scaled = 0.75 * RADIUS * inverse
    along = jnp.where(same, jnp.float32(1.0), scaled * (1.0 + 2.0 / 3.0 * RADIUS * RADIUS * inv_sq))
    across = jnp.where(
        same, jnp.float32(0.0), scaled * inv_sq * (1.0 - 2.0 * RADIUS * RADIUS * inv_sq)
    )
    identity = jnp.eye(3, dtype=jnp.float32)
    return (
        identity[:, :, None, None] * along[None, None]
        + delta[:, None] * (across[None] * delta)[None]
    )


def gathered(positions, probes):
    seg_len = positions.shape[1]
    probe_count = probes.shape[1]
    n_row = lax.axis_size("row")
    n_col = lax.axis_size("col")
    beads_all = seg_len * n_row * n_col
    places = lax.all_gather(positions, ("row", "col"), axis=1, tiled=True)
    all_ids = jnp.arange(beads_all, dtype=jnp.int32)
    own_at = (lax.axis_index("row") * n_col + lax.axis_index("col")) * seg_len
    own_ids = own_at + jnp.arange(seg_len, dtype=jnp.int32)
    width = block_width(beads_all)

    def apply_mobility(vectors):
        whole = lax.all_gather(vectors, ("row", "col"), axis=2, tiled=True)

        def add_block(block_step, carried):
            offset = block_step * width
            cols_pos = lax.dynamic_slice_in_dim(places, offset, width, 1)
            cols_ids = lax.dynamic_slice_in_dim(all_ids, offset, width, 0)
            mobility = mobility_block(positions, own_ids, cols_pos, cols_ids)
            columns = lax.dynamic_slice_in_dim(whole, offset, width, 2)
            image = carried[0] + jnp.einsum(
                "abrc,bpc->apr", mobility, columns, precision=lax.Precision.HIGHEST
            )
            return image, carried[1] + jnp.sum(jnp.abs(mobility), axis=(1, 3))

        zeros = (jnp.zeros((3, probe_count, seg_len), F32), jnp.zeros((3, seg_len), F32))
        return lax.fori_loop(0, beads_all // width, add_block, zeros)

    image, row_sums = apply_mobility(probes)
    ceiling = lax.pmax(jnp.max(row_sums), ("row", "col"))
    factor = 2.0 / ceiling
    previous = probes
    current = factor * image - probes
    noise_sum = cheb_weight(0) * previous + cheb_weight(1) * current
    for degree_step in range(2, DEG + 1):
        following = 2.0 * (factor * apply_mobility(current)[0] - current) - previous
        previous, current = (current, following)
        noise_sum = noise_sum + cheb_weight(degree_step) * current
    return jnp.sqrt(ceiling) * noise_sum


def solution(mesh):
    split_by = ("groups", "row", "col")
    square = mesh.shape["row"] == 4 and mesh.shape["col"] == 4

    def per_device(positions, probes):
        if square and probes.shape == (3, 16, 64):
            return fused(positions, probes)
        return gathered(positions, probes)

    return jax.shard_map(
        per_device,
        mesh=mesh,
        in_specs=(P(None, split_by), P(None, None, split_by)),
        out_specs=P(None, None, split_by),
        check_vma=False,
    )
```

```python
import functools
import math

import jax
import jax.numpy as jnp
from jax import lax
from jax.experimental import pallas as pl
from jax.experimental.pallas import tpu as pltpu
from jax.sharding import PartitionSpec as P

DEG = 4
RADIUS = 0.3
MESH = pl.DeviceIdType.MESH
F32 = jnp.float32
BF16 = jnp.bfloat16


def cheb_weight(degree_step):
    if degree_step == 0:
        return 2.0 / math.pi
    return 4.0 * (-1.0) ** (degree_step + 1) / (math.pi * (4.0 * degree_step * degree_step - 1.0))


def flips(index):
    third = 3 - index
    return [index, lax.rem(third + 2, 4), lax.rem(index + 2, 4), third]


def split(value):
    high = value.astype(BF16)
    return high, (value - high.astype(F32)).astype(BF16)


def kernel(
    pos_hbm, probes_hbm, out_ref,
    pos_ref, probes_ref, msg, first, field, posT, w_high, w_low, gather, last_out, last_in,
    load, row_send, row_recv, first_send, first_recv, gather_send, gather_recv, last_send, last_recv,
):
    row = lax.axis_index("row")
    col = lax.axis_index("col")
    rows_by, cols_by = flips(row), flips(col)
    partners = [(2, 0), (3, 0), (1, 0), (0, 2), (0, 3), (0, 1)]

    loads = [
        pltpu.make_async_copy(pos_hbm, pos_ref, load.at[0]),
        pltpu.make_async_copy(probes_hbm, probes_ref, load.at[1]),
    ]
    barrier = pltpu.get_barrier_semaphore()
    for dr, dc in partners:
        pl.semaphore_signal(
            barrier, inc=1, device_id={"row": rows_by[dr], "col": cols_by[dc]}, device_id_type=MESH
        )
    for copy in loads:
        copy.start()
    for copy in loads:
        copy.wait()

    scaled_pos = pos_ref[...] * (1.0 / (0.75 * RADIUS))
    for r in range(4):
        mine = [probes_ref[t, 4 * r : 4 * r + 4, :] for t in range(3)]
        left = jnp.concatenate([mine[0], mine[1]], axis=0)
        right = jnp.concatenate([mine[2], scaled_pos, jnp.ones((1, 64), F32)], axis=0)
        msg[r] = jnp.concatenate([left, right], axis=1)
    first[0, 0] = msg[row]

    pl.semaphore_wait(barrier, len(partners))
    row_copies = {}
    for dr in (2, 3, 1):
        row_copies[dr] = pltpu.make_async_remote_copy(
            src_ref=msg.at[rows_by[dr]],
            dst_ref=first.at[0, dr],
            send_sem=row_send.at[dr],
            recv_sem=row_recv.at[dr],
            device_id={"row": rows_by[dr], "col": col},
            device_id_type=MESH,
        )
        row_copies[dr].start()

    low_lanes = lax.broadcasted_iota(jnp.int32, (8, 128), 1) < 64

    def unpack(dc):
        for h in range(2):
            even, odd = first[dc, 2 * h], first[dc, 2 * h + 1]
            lanes = slice(128 * h, 128 * h + 128)
            field[dc, 0:8, lanes] = jnp.where(low_lanes, even, pltpu.roll(odd, 64, 1))
            field[dc, 8:16, lanes] = jnp.where(low_lanes, pltpu.roll(even, 64, 1), odd)
        pair = jnp.concatenate([field[dc, 8:16, 0:128], field[dc, 8:16, 128:256]], axis=0)
        posT[dc] = pair.T

    unit = (0.75 * RADIUS) ** 2
    c_along = 2.0 / 3.0 * RADIUS * RADIUS / unit
    c_across = 2.0 * RADIUS * RADIUS / unit
    STEP = 16
    own_bead = lax.broadcasted_iota(jnp.int32, (STEP, 128), 1)
    step_bead = lax.broadcasted_iota(jnp.int32, (STEP, 128), 0)

    def generate(dc, h, sums):
        sums = [list(half) for half in sums]
        for at in range(0, 128, STEP):
            rows = slice(256 * dc + 128 * h + at, 256 * dc + 128 * h + at + STEP)
            centres = posT[dc, at : at + STEP, :]
            centres = [centres[:, 8 * h + 4 + t : 8 * h + 5 + t] for t in range(3)]
            centres = [jnp.broadcast_to(c, (STEP, 128)) for c in centres]
            for own in range(2):
                d = [field[0, 12 + t : 13 + t, 128 * own : 128 * own + 128] - centres[t] for t in range(3)]
                dist_sq = d[0] * d[0] + d[1] * d[1] + d[2] * d[2]
                diagonal = dc == 0 and own == h
                if diagonal:
                    same = (step_bead + at) == own_bead
                    dist_sq = jnp.where(same, 1.0, dist_sq)
                inverse = lax.rsqrt(dist_sq)
                inv_sq = inverse * inverse
                cubed = inverse * inv_sq
                along = inverse + c_along * cubed
                across = cubed - c_across * (cubed * inv_sq)
                if diagonal:
                    along = jnp.where(same, 1.0, along)
                    across = jnp.where(same, 0.0, across)
                g = [across * d[t] for t in range(3)]
                parts = [
                    along + g[0] * d[0], along + g[1] * d[1], along + g[2] * d[2],
                    g[0] * d[1], g[0] * d[2], g[1] * d[2],
                ]
                for k, part in enumerate(parts):
                    high, low = split(part)
                    lanes = slice(768 * own + 128 * k, 768 * own + 128 * k + 128)
                    w_high[rows, lanes] = high
                    w_low[rows, lanes] = low
                for t in range(3):
                    mag = jnp.abs(parts[3 + t])
                    sums[own][t] = sums[own][t] + (mag[0:8] + mag[8:16])
        return tuple(tuple(half) for half in sums)

    def multiply(blocks, dc):
        rows = slice(256 * dc, 256 * (dc + len(blocks)))
        high, low = split(jnp.concatenate(blocks, axis=1))
        both = jnp.concatenate([high, low], axis=0)
        image = jnp.dot(both, w_high[rows, :], preferred_element_type=F32)
        rest = jnp.dot(high, w_low[rows, :], preferred_element_type=F32)
        return image[0:16] + image[16:32] + rest

    def combine(acc):
        packed = []
        at = {"x": (0, 3, 4), "y": (3, 1, 5), "z": (4, 5, 2)}
        for component in "xyz":
            for own in range(2):
                terms = [
                    acc[4 * t : 4 * t + 4, 768 * own + 128 * k : 768 * own + 128 * k + 128]
                    for t, k in enumerate(at[component])
                ]
                packed.append(terms[0] + terms[1] + terms[2])
        return jnp.concatenate(packed, axis=0)

    def pack(block):
        return jnp.concatenate(
            [block[4 * t : 4 * t + 4, 128 * h : 128 * h + 128] for t in range(3) for h in range(2)], axis=0
        )

    def unpacked(packed):
        return jnp.concatenate(
            [
                jnp.concatenate(
                    [packed[8 * t + 4 * h : 8 * t + 4 * h + 4] for t in range(3)] + [jnp.zeros((4, 128), F32)],
                    axis=0,
                )
                for h in range(2)
            ],
            axis=1,
        )

    gather_copies = {}

    def send(k, value):
        rows = slice(0, value.shape[0])
        gather[k, 0, rows] = value
        for dc in (3, 2, 1):
            gather_copies[k, dc] = pltpu.make_async_remote_copy(
                src_ref=gather.at[k, 0, rows],
                dst_ref=gather.at[k, dc, rows],
                send_sem=gather_send.at[k, dc],
                recv_sem=gather_recv.at[k, dc],
                device_id={"row": row, "col": cols_by[dc]},
                device_id_type=MESH,
            )
            gather_copies[k, dc].start()

    def apply(k):
        acc = multiply([unpacked(gather[k, 0, 0:24])], 0)
        for dc in range(1, 4):
            gather_copies[k, dc].wait_recv()
        return combine(acc + multiply([unpacked(gather[k, dc, 0:24]) for dc in range(1, 4)], 1))

    for dr in (1, 2, 3):
        row_copies[dr].wait_recv()
    first_copies = {}
    for dc in (2, 3, 1):
        first_copies[dc] = pltpu.make_async_remote_copy(
            src_ref=first.at[0],
            dst_ref=first.at[dc],
            send_sem=first_send.at[dc],
            recv_sem=first_recv.at[dc],
            device_id={"row": row, "col": cols_by[dc]},
            device_id_type=MESH,
        )
        first_copies[dc].start()
    unpack(0)
    sums = tuple(tuple(jnp.zeros((8, 128), F32) for _ in range(3)) for _ in range(2))
    sums = generate(0, 0, sums)
    sums = generate(0, 1, sums)
    for dc in range(1, 4):
        first_copies[dc].wait_recv()
    for dc in range(1, 4):
        unpack(dc)

    acc = None
    for dc in range(1, 4):
        sums = generate(dc, 0, sums)
        term = multiply([field[dc - 1]], dc - 1)
        acc = term if acc is None else acc + term
        sums = generate(dc, 1, sums)
    acc = acc + multiply([field[3]], 3)
    image1 = combine(acc)
    row_max = None
    for own in range(2):
        xx, yy, zz = [acc[15:16, 768 * own + 128 * k : 768 * own + 128 * k + 128] for k in range(3)]
        xy, xz, yz = [jnp.sum(s, axis=0, keepdims=True) for s in sums[own]]
        largest = jnp.maximum(jnp.maximum(xx + xy + xz, xy + yy + yz), xz + yz + zz)
        row_max = largest if row_max is None else jnp.maximum(row_max, largest)
    row_max = jnp.max(row_max, axis=1, keepdims=True)
    send(0, jnp.concatenate([image1, jnp.broadcast_to(row_max, (8, 128))], axis=0))
    start = pack(field[0])
    image2 = apply(0)
    top = functools.reduce(jnp.maximum, [gather[0, dc, 24:25, :] for dc in range(4)])
    factor = 2.0 / top
    basis1 = factor * image1 - start
    basis2 = 2.0 * (factor * (factor * image2 - image1) - basis1) - start
    send(1, basis2)
    noise = cheb_weight(0) * start + cheb_weight(1) * basis1 + cheb_weight(2) * basis2
    basis3 = 2.0 * (factor * apply(1) - basis2) - basis1
    send(2, basis3)
    noise = noise + cheb_weight(3) * basis3
    basis4 = 2.0 * (factor * apply(2) - basis3) - basis2
    noise = unpacked(jnp.sqrt(top) * (noise + cheb_weight(4) * basis4))

    last_copies = []
    for dr in (2, 3, 1, 0):
        h = dr // 2
        upper = noise[0:8, 128 * h : 128 * h + 128]
        lower = noise[8:16, 128 * h : 128 * h + 128]
        if dr % 2 == 0:
            tile = jnp.where(low_lanes, upper, pltpu.roll(lower, 64, 1))
        else:
            tile = jnp.where(low_lanes, pltpu.roll(upper, 64, 1), lower)
        if dr == 0:
            last_in[row] = tile
        else:
            last_out[dr] = tile
            copy = pltpu.make_async_remote_copy(
                src_ref=last_out.at[dr],
                dst_ref=last_in.at[row],
                send_sem=last_send.at[dr],
                recv_sem=last_recv.at[dr],
                device_id={"row": rows_by[dr], "col": col},
                device_id_type=MESH,
            )
            copy.start()
            last_copies.append(copy)
    for copy in [*row_copies.values(), *first_copies.values()]:
        copy.wait_send()
    for copy in gather_copies.values():
        copy.wait_send()
    for copy in last_copies:
        copy.wait()
    for q in range(4):
        tile = last_in[q]
        out_ref[0, 4 * q : 4 * q + 4, :] = tile[0:4, 0:64]
        out_ref[1, 4 * q : 4 * q + 4, :] = tile[4:8, 0:64]
        out_ref[2, 4 * q : 4 * q + 4, :] = tile[0:4, 64:128]


def fused(positions, probes):
    DMA = pltpu.SemaphoreType.DMA
    return pl.pallas_call(
        kernel,
        out_shape=jax.ShapeDtypeStruct(probes.shape, F32),
        in_specs=[pl.BlockSpec(memory_space=pltpu.HBM)] * 2,
        out_specs=pl.BlockSpec(memory_space=pltpu.VMEM),
        scratch_shapes=[
            pltpu.VMEM(positions.shape, F32),
            pltpu.VMEM(probes.shape, F32),
            pltpu.VMEM((4, 8, 128), F32),
            pltpu.VMEM((4, 4, 8, 128), F32),
            pltpu.VMEM((4, 16, 256), F32),
            pltpu.VMEM((4, 128, 16), F32),
            pltpu.VMEM((1024, 1536), BF16),
            pltpu.VMEM((1024, 1536), BF16),
            pltpu.VMEM((DEG - 1, 4, 32, 128), F32),
            pltpu.VMEM((4, 8, 128), F32),
            pltpu.VMEM((4, 8, 128), F32),
            DMA((2,)),
            DMA((4,)),
            DMA((4,)),
            DMA((4,)),
            DMA((4,)),
            DMA((DEG - 1, 4)),
            DMA((DEG - 1, 4)),
            DMA((4,)),
            DMA((4,)),
        ],
        compiler_params=pltpu.CompilerParams(
            collective_id=0, has_side_effects=True, vmem_limit_bytes=32 * 1024 * 1024
        ),
        name="fused",
    )(*[pltpu.with_memory_space_constraint(x, pltpu.HBM) for x in (positions, probes)])


def block_width(length):
    width = min(length, 512)
    while length % width != 0:
        width = width - 1
    return width


def mobility_block(rows_pos, rows_ids, cols_pos, cols_ids):
    delta = rows_pos[:, :, None] - cols_pos[:, None, :]
    dist_sq = jnp.sum(delta * delta, axis=0)
    same = rows_ids[:, None] == cols_ids[None, :]
    inverse = lax.rsqrt(dist_sq + same.astype(jnp.float32))
    inv_sq = inverse * inverse
    scaled = 0.75 * RADIUS * inverse
    along = jnp.where(same, jnp.float32(1.0), scaled * (1.0 + 2.0 / 3.0 * RADIUS * RADIUS * inv_sq))
    across = jnp.where(
        same, jnp.float32(0.0), scaled * inv_sq * (1.0 - 2.0 * RADIUS * RADIUS * inv_sq)
    )
    identity = jnp.eye(3, dtype=jnp.float32)
    return (
        identity[:, :, None, None] * along[None, None]
        + delta[:, None] * (across[None] * delta)[None]
    )


def gathered(positions, probes):
    seg_len = positions.shape[1]
    probe_count = probes.shape[1]
    n_row = lax.axis_size("row")
    n_col = lax.axis_size("col")
    beads_all = seg_len * n_row * n_col
    places = lax.all_gather(positions, ("row", "col"), axis=1, tiled=True)
    all_ids = jnp.arange(beads_all, dtype=jnp.int32)
    own_at = (lax.axis_index("row") * n_col + lax.axis_index("col")) * seg_len
    own_ids = own_at + jnp.arange(seg_len, dtype=jnp.int32)
    width = block_width(beads_all)

    def apply_mobility(vectors):
        whole = lax.all_gather(vectors, ("row", "col"), axis=2, tiled=True)

        def add_block(block_step, carried):
            offset = block_step * width
            cols_pos = lax.dynamic_slice_in_dim(places, offset, width, 1)
            cols_ids = lax.dynamic_slice_in_dim(all_ids, offset, width, 0)
            mobility = mobility_block(positions, own_ids, cols_pos, cols_ids)
            columns = lax.dynamic_slice_in_dim(whole, offset, width, 2)
            image = carried[0] + jnp.einsum(
                "abrc,bpc->apr", mobility, columns, precision=lax.Precision.HIGHEST
            )
            return image, carried[1] + jnp.sum(jnp.abs(mobility), axis=(1, 3))

        zeros = (jnp.zeros((3, probe_count, seg_len), F32), jnp.zeros((3, seg_len), F32))
        return lax.fori_loop(0, beads_all // width, add_block, zeros)

    image, row_sums = apply_mobility(probes)
    ceiling = lax.pmax(jnp.max(row_sums), ("row", "col"))
    factor = 2.0 / ceiling
    previous = probes
    current = factor * image - probes
    noise_sum = cheb_weight(0) * previous + cheb_weight(1) * current
    for degree_step in range(2, DEG + 1):
        following = 2.0 * (factor * apply_mobility(current)[0] - current) - previous
        previous, current = (current, following)
        noise_sum = noise_sum + cheb_weight(degree_step) * current
    return jnp.sqrt(ceiling) * noise_sum


def solution(mesh):
    split_by = ("groups", "row", "col")
    square = mesh.shape["row"] == 4 and mesh.shape["col"] == 4

    def per_device(positions, probes):
        if square and probes.shape == (3, 16, 64):
            return fused(positions, probes)
        return gathered(positions, probes)

    return jax.shard_map(
        per_device,
        mesh=mesh,
        in_specs=(P(None, split_by), P(None, None, split_by)),
        out_specs=P(None, None, split_by),
        check_vma=False,
    )
```

```python
import functools
import math

import jax
import jax.numpy as jnp
from jax import lax
from jax.experimental import pallas as pl
from jax.experimental.pallas import tpu as pltpu
from jax.sharding import PartitionSpec as P

DEG = 4
RADIUS = 0.3
MESH = pl.DeviceIdType.MESH
F32 = jnp.float32
BF16 = jnp.bfloat16


def cheb_weight(degree_step):
    if degree_step == 0:
        return 2.0 / math.pi
    return 4.0 * (-1.0) ** (degree_step + 1) / (math.pi * (4.0 * degree_step * degree_step - 1.0))


def flip(index, bits):
    for bit in (1, 2, 4, 8):
        if bits & bit:
            index = index + bit - 2 * bit * lax.rem(lax.div(index, bit), 2)
    return index


def split(value):
    high = value.astype(BF16)
    return high, (value - high.astype(F32)).astype(BF16)


def kernel(
    pos_hbm, probes_hbm, out_ref,
    pos_ref, probes_ref, msg, first, field, posT, w_high, w_low, gather, last_out, last_in,
    load, first_send, first_recv, gather_send, gather_recv, last_send, last_recv,
):
    row = lax.axis_index("row")
    col = lax.axis_index("col")
    partners = [(dr, dc) for dc in range(4) for dr in (2, 3, 1, 0) if (dr, dc) != (0, 0)]

    loads = [
        pltpu.make_async_copy(pos_hbm, pos_ref, load.at[0]),
        pltpu.make_async_copy(probes_hbm, probes_ref, load.at[1]),
    ]
    for copy in loads:
        copy.start()
    barrier = pltpu.get_barrier_semaphore()
    for dr, dc in partners:
        pl.semaphore_signal(
            barrier, inc=1, device_id={"row": flip(row, dr), "col": flip(col, dc)}, device_id_type=MESH
        )
    for copy in loads:
        copy.wait()

    scaled_pos = pos_ref[...] * (1.0 / (0.75 * RADIUS))
    for r in range(4):
        mine = [probes_ref[t, 4 * r : 4 * r + 4, :] for t in range(3)]
        left = jnp.concatenate([mine[0], mine[1]], axis=0)
        right = jnp.concatenate([mine[2], scaled_pos, jnp.zeros((1, 64), F32)], axis=0)
        msg[r] = jnp.concatenate([left, right], axis=1)
    first[0, 0] = msg[row]

    pl.semaphore_wait(barrier, len(partners))
    first_copies = {}
    for dr, dc in partners:
        to_row = flip(row, dr)
        copy = pltpu.make_async_remote_copy(
            src_ref=msg.at[to_row],
            dst_ref=first.at[dc, dr],
            send_sem=first_send.at[dc, dr],
            recv_sem=first_recv.at[dc, dr],
            device_id={"row": to_row, "col": flip(col, dc)},
            device_id_type=MESH,
        )
        copy.start()
        first_copies[dc, dr] = copy

    def to_col(source, target, dc, send_sem, recv_sem):
        copy = pltpu.make_async_remote_copy(
            src_ref=source,
            dst_ref=target,
            send_sem=send_sem,
            recv_sem=recv_sem,
            device_id={"row": row, "col": flip(col, dc)},
            device_id_type=MESH,
        )
        copy.start()
        return copy

    low_lanes = lax.broadcasted_iota(jnp.int32, (8, 128), 1) < 64

    def unpack(dc):
        for h in range(2):
            even, odd = first[dc, 2 * h], first[dc, 2 * h + 1]
            field[dc, h, 0:8] = jnp.where(low_lanes, even, pltpu.roll(odd, 64, 1))
            field[dc, h, 8:16] = jnp.where(low_lanes, pltpu.roll(even, 64, 1), odd)
        pair = jnp.concatenate([field[dc, 0, 8:16], field[dc, 1, 8:16]], axis=0)
        posT[dc] = pair.T

    pairs = [((0, 0), (0, 1)), ((1, 1), (2, 1)), ((3, 1), (1, 0)), ((2, 0), (3, 0))]
    place = {half: (block, at) for block, pair in enumerate(pairs) for at, half in enumerate(pair)}

    unit = (0.75 * RADIUS) ** 2
    c_along = 2.0 / 3.0 * RADIUS * RADIUS / unit
    c_across = 2.0 * RADIUS * RADIUS / unit
    STEP = 16
    own_bead = lax.broadcasted_iota(jnp.int32, (STEP, 128), 1)
    step_bead = lax.broadcasted_iota(jnp.int32, (STEP, 128), 0)
    sums = [[jnp.zeros((8, 128), F32) for _ in range(3)] for _ in range(2)]

    def generate(dc, h):
        block, part_at = place[dc, h]
        for at in range(0, 128, STEP):
            rows = slice(128 * part_at + at, 128 * part_at + at + STEP)
            centres = [posT[dc, at : at + STEP, 8 * h + 4 + t : 8 * h + 5 + t] for t in range(3)]
            centres = [jnp.broadcast_to(c, (STEP, 128)) for c in centres]
            for own in range(2):
                d = [field[0, own, 12 + t : 13 + t, :] - centres[t] for t in range(3)]
                dist_sq = d[0] * d[0] + d[1] * d[1] + d[2] * d[2]
                diagonal = dc == 0 and own == h
                if diagonal:
                    same = (step_bead + at) == own_bead
                    dist_sq = jnp.where(same, 1.0, dist_sq)
                inverse = lax.rsqrt(dist_sq)
                inv_sq = inverse * inverse
                cubed = inverse * inv_sq
                along = inverse + c_along * cubed
                across = cubed - c_across * (cubed * inv_sq)
                if diagonal:
                    along = jnp.where(same, 1.0, along)
                    across = jnp.where(same, 0.0, across)
                g = [across * d[t] for t in range(3)]
                parts = [
                    along + g[0] * d[0], along + g[1] * d[1], along + g[2] * d[2],
                    g[0] * d[1], g[0] * d[2], g[1] * d[2],
                ]
                for k, part in enumerate(parts):
                    high, low = split(part)
                    lanes = slice(768 * own + 128 * k, 768 * own + 128 * k + 128)
                    w_high[block, rows, lanes] = high
                    w_low[block, rows, lanes] = low
                mags = [jnp.abs(part) for part in parts]
                mags = [mag[0:8] + mag[8:16] for mag in mags]
                for t, (p, q, r) in enumerate(((0, 3, 4), (1, 3, 5), (2, 4, 5))):
                    sums[own][t] = sums[own][t] + (mags[p] + mags[q] + mags[r])

    def multiply(parts, block, own):
        high, low = parts
        lanes = slice(768 * own, 768 * own + 768)
        both = jnp.concatenate([high, low], axis=0)
        image = jnp.dot(both, w_high[block, :, lanes], preferred_element_type=F32)
        rest = jnp.dot(high, w_low[block, :, lanes], preferred_element_type=F32)
        return image[0:16] + image[16:32] + rest

    def combine(acc):
        xx, yy, zz, xy, xz, yz = [acc[:, 128 * k : 128 * k + 128] for k in range(6)]
        return jnp.concatenate(
            [
                xx[0:4] + xy[4:8] + xz[8:12],
                xy[0:4] + yy[4:8] + yz[8:12],
                xz[0:4] + yz[4:8] + zz[8:12],
            ],
            axis=0,
        )

    def operand(halves, block):
        return split(jnp.concatenate([halves(*half) for half in pairs[block]], axis=1))

    gather_copies = {}

    def send(k, own, value, rest):
        gather[k, 0, own] = jnp.concatenate([value, rest], axis=0)
        for dc in (2, 3, 1):
            gather_copies[k, dc, own] = to_col(
                gather.at[k, 0, own], gather.at[k, dc, own], dc,
                gather_send.at[k, dc, own], gather_recv.at[k, dc, own],
            )

    def images(k):
        acc = [None, None]
        for block in range(4):
            for dc, h in pairs[block]:
                if dc:
                    gather_copies[k, dc, h].wait_recv()
            parts = operand(lambda dc, h: gather[k, dc, h], block)
            for own in (1, 0):
                term = multiply(parts, block, own)
                acc[own] = term if block == 0 else acc[own] + term
                if block == 3:
                    yield own, combine(acc[own])

    for dr in (1, 2, 3):
        first_copies[0, dr].wait_recv()
    unpack(0)
    generate(0, 0)
    generate(0, 1)
    for dc in range(1, 4):
        for dr in range(4):
            first_copies[dc, dr].wait_recv()
    for dc in range(1, 4):
        unpack(dc)

    def field_half(dc, h):
        return field[dc, h]

    acc = [None, None]
    for block in range(4):
        if block < 3:
            generate(*pairs[block + 1][0])
        else:
            row_max = functools.reduce(
                jnp.maximum, [jnp.sum(s, axis=0, keepdims=True) for half in sums for s in half]
            )
            row_max = jnp.broadcast_to(jnp.max(row_max, axis=1, keepdims=True), (4, 128))
        parts = operand(field_half, block)
        for own in (1, 0):
            term = multiply(parts, block, own)
            acc[own] = term if block == 0 else acc[own] + term
            if block == 3:
                acc[own] = combine(acc[own])
                send(0, own, acc[own], row_max)
        if block < 3:
            generate(*pairs[block + 1][1])
    image1 = acc

    pad = jnp.zeros((4, 128), F32)
    start = [field[0, own, 0:12, :] for own in range(2)]
    basis1, basis2, basis3, noise = [None, None], [None, None], [None, None], [None, None]
    factor = top = None
    for own, image2 in images(0):
        if factor is None:
            top = functools.reduce(jnp.maximum, [gather[0, dc, 1, 12:13, :] for dc in range(4)])
            factor = 2.0 / top
        basis1[own] = factor * image1[own] - start[own]
        basis2[own] = 2.0 * (factor * (factor * image2 - image1[own]) - basis1[own]) - start[own]
        send(1, own, basis2[own], pad)
    for own, image3 in images(1):
        basis3[own] = 2.0 * (factor * image3 - basis2[own]) - basis1[own]
        send(2, own, basis3[own], pad)
    for own in range(2):
        noise[own] = cheb_weight(0) * start[own] + cheb_weight(1) * basis1[own]
        noise[own] = noise[own] + cheb_weight(2) * basis2[own] + cheb_weight(3) * basis3[own]

    last_copies = []
    root = jnp.sqrt(top)
    for own, image4 in images(2):
        basis4 = 2.0 * (factor * image4 - basis3[own]) - basis2[own]
        result = root * (noise[own] + cheb_weight(4) * basis4)
        upper, lower = result[0:8], jnp.concatenate([result[8:12], pad], axis=0)
        for dr in (2 * own, 2 * own + 1):
            if dr % 2 == 0:
                tile = jnp.where(low_lanes, upper, pltpu.roll(lower, 64, 1))
            else:
                tile = jnp.where(low_lanes, pltpu.roll(upper, 64, 1), lower)
            if dr == 0:
                last_in[row] = tile
                continue
            last_out[dr] = tile
            copy = pltpu.make_async_remote_copy(
                src_ref=last_out.at[dr],
                dst_ref=last_in.at[row],
                send_sem=last_send.at[dr],
                recv_sem=last_recv.at[dr],
                device_id={"row": flip(row, dr), "col": col},
                device_id_type=MESH,
            )
            copy.start()
            last_copies.append(copy)
    for copy in [*first_copies.values(), *gather_copies.values()]:
        copy.wait_send()
    for copy in last_copies:
        copy.wait()
    for q in range(4):
        tile = last_in[q]
        out_ref[0, 4 * q : 4 * q + 4, :] = tile[0:4, 0:64]
        out_ref[1, 4 * q : 4 * q + 4, :] = tile[4:8, 0:64]
        out_ref[2, 4 * q : 4 * q + 4, :] = tile[0:4, 64:128]


def fused(positions, probes):
    DMA = pltpu.SemaphoreType.DMA
    return pl.pallas_call(
        kernel,
        out_shape=jax.ShapeDtypeStruct(probes.shape, F32),
        in_specs=[pl.BlockSpec(memory_space=pltpu.HBM)] * 2,
        out_specs=pl.BlockSpec(memory_space=pltpu.VMEM),
        scratch_shapes=[
            pltpu.VMEM(positions.shape, F32),
            pltpu.VMEM(probes.shape, F32),
            pltpu.VMEM((4, 8, 128), F32),
            pltpu.VMEM((4, 4, 8, 128), F32),
            pltpu.VMEM((4, 2, 16, 128), F32),
            pltpu.VMEM((4, 128, 16), F32),
            pltpu.VMEM((4, 256, 1536), BF16),
            pltpu.VMEM((4, 256, 1536), BF16),
            pltpu.VMEM((DEG - 1, 4, 2, 16, 128), F32),
            pltpu.VMEM((4, 8, 128), F32),
            pltpu.VMEM((4, 8, 128), F32),
            DMA((2,)),
            DMA((4, 4)),
            DMA((4, 4)),
            DMA((DEG - 1, 4, 2)),
            DMA((DEG - 1, 4, 2)),
            DMA((4,)),
            DMA((4,)),
        ],
        compiler_params=pltpu.CompilerParams(
            collective_id=0, has_side_effects=True, vmem_limit_bytes=32 * 1024 * 1024
        ),
        name="fused",
    )(*[pltpu.with_memory_space_constraint(x, pltpu.HBM) for x in (positions, probes)])


def block_width(length):
    width = min(length, 512)
    while length % width != 0:
        width = width - 1
    return width


def mobility_block(rows_pos, rows_ids, cols_pos, cols_ids):
    delta = rows_pos[:, :, None] - cols_pos[:, None, :]
    dist_sq = jnp.sum(delta * delta, axis=0)
    same = rows_ids[:, None] == cols_ids[None, :]
    inverse = lax.rsqrt(dist_sq + same.astype(jnp.float32))
    inv_sq = inverse * inverse
    scaled = 0.75 * RADIUS * inverse
    along = jnp.where(same, jnp.float32(1.0), scaled * (1.0 + 2.0 / 3.0 * RADIUS * RADIUS * inv_sq))
    across = jnp.where(
        same, jnp.float32(0.0), scaled * inv_sq * (1.0 - 2.0 * RADIUS * RADIUS * inv_sq)
    )
    identity = jnp.eye(3, dtype=jnp.float32)
    return (
        identity[:, :, None, None] * along[None, None]
        + delta[:, None] * (across[None] * delta)[None]
    )


def gathered(positions, probes):
    seg_len = positions.shape[1]
    probe_count = probes.shape[1]
    n_row = lax.axis_size("row")
    n_col = lax.axis_size("col")
    beads_all = seg_len * n_row * n_col
    places = lax.all_gather(positions, ("row", "col"), axis=1, tiled=True)
    all_ids = jnp.arange(beads_all, dtype=jnp.int32)
    own_at = (lax.axis_index("row") * n_col + lax.axis_index("col")) * seg_len
    own_ids = own_at + jnp.arange(seg_len, dtype=jnp.int32)
    width = block_width(beads_all)

    def apply_mobility(vectors):
        whole = lax.all_gather(vectors, ("row", "col"), axis=2, tiled=True)

        def add_block(block_step, carried):
            offset = block_step * width
            cols_pos = lax.dynamic_slice_in_dim(places, offset, width, 1)
            cols_ids = lax.dynamic_slice_in_dim(all_ids, offset, width, 0)
            mobility = mobility_block(positions, own_ids, cols_pos, cols_ids)
            columns = lax.dynamic_slice_in_dim(whole, offset, width, 2)
            image = carried[0] + jnp.einsum(
                "abrc,bpc->apr", mobility, columns, precision=lax.Precision.HIGHEST
            )
            return image, carried[1] + jnp.sum(jnp.abs(mobility), axis=(1, 3))

        zeros = (jnp.zeros((3, probe_count, seg_len), F32), jnp.zeros((3, seg_len), F32))
        return lax.fori_loop(0, beads_all // width, add_block, zeros)

    image, row_sums = apply_mobility(probes)
    ceiling = lax.pmax(jnp.max(row_sums), ("row", "col"))
    factor = 2.0 / ceiling
    previous = probes
    current = factor * image - probes
    noise_sum = cheb_weight(0) * previous + cheb_weight(1) * current
    for degree_step in range(2, DEG + 1):
        following = 2.0 * (factor * apply_mobility(current)[0] - current) - previous
        previous, current = (current, following)
        noise_sum = noise_sum + cheb_weight(degree_step) * current
    return jnp.sqrt(ceiling) * noise_sum


def solution(mesh):
    split_by = ("groups", "row", "col")
    square = mesh.shape["row"] == 4 and mesh.shape["col"] == 4

    def per_device(positions, probes):
        if square and probes.shape == (3, 16, 64):
            return fused(positions, probes)
        return gathered(positions, probes)

    return jax.shard_map(
        per_device,
        mesh=mesh,
        in_specs=(P(None, split_by), P(None, None, split_by)),
        out_specs=P(None, None, split_by),
        check_vma=False,
    )
```
